32 devices in a mesh: rows: 2 (over x), query: 16 (over z, y, core).
Axes of the slice: x: 2, y: 2, z: 4, core: 2. Of those that a mesh axis runs over, the one named last changes fastest.
Arguments:
- acts: bfloat16 [640, 28672], P('query', 'rows'), may hold values from -6 to 6
- grads: bfloat16 [640, 8192], P('query', 'rows'), may hold values from -6 to 6
- in_factors: bfloat16 [28672, 8192], P('rows', 'query')
- out_factors: bfloat16 [8192, 8192], P('rows', 'query')
Outputs:
- scores: float32 [640, 256], P('rows', 'query')
The draws below stay inside these ranges and needn't reach their ends.
All inputs are finite; a program needn't handle non-finite values.
Results may differ from the reference program's by a relative error of at most 0.0003.
Values may be sent and summed in bfloat16 or wider, within the bound.
No kernel may reach another device: no remote copies, remote signals or barrier semaphores. Data moves between devices by JAX's collectives and lax.ppermute only.
A program may use at most 128 MiB of HBM per device.

```python
import math
import jax
import jax.numpy as jnp
from jax import lax

D = 8192
FF = 28672
RANK = 32
QUERIES = 256
TOKENS = 640


def factor_draw(key, count_rows, count_cols):
    first, second, third = jax.random.split(key, 3)
    base = jax.random.normal(first, (count_rows, count_cols), jnp.float32)
    row_scale = jnp.exp(jax.random.uniform(second, (count_rows, 1), jnp.float32, 0.0, math.log(10.0)))
    col_scale = jnp.exp(jax.random.uniform(third, (1, count_cols), jnp.float32, 0.0, math.log(10.0)))
    ramp = jnp.exp(math.log(3.0) * jnp.arange(count_rows, dtype=jnp.float32) / count_rows)[:, None]
    values = base * row_scale * col_scale * ramp / (40.0 * math.sqrt(count_rows))
    return values.astype(jnp.bfloat16)


def draw_in_factors(key, part):
    return factor_draw(jax.random.fold_in(key, 11), FF, QUERIES * RANK)


def draw_out_factors(key, part):
    return factor_draw(jax.random.fold_in(key, 23), D, QUERIES * RANK)


def raised(entries, own_key, source, target, parts, factor):
    owner, partner = [(jnp.arange(entries.shape[dim]) // (entries.shape[dim] // parts)).reshape([-1 if axis == dim else 1 for axis in range(entries.ndim)]) for dim in (source, target)]
    chosen = jax.random.permutation(own_key, parts)[partner]
    strong = (owner == chosen) | (owner == (partner + parts // 2) % parts)
    return jnp.where(strong, factor * entries, entries)


def level_of(key, shape, cuts, least, top_value):
    loudness, own = 1.0, jax.random.fold_in(key, 6)
    for axis_at, blocks in cuts:
        steps = jnp.exp(jax.random.uniform(jax.random.fold_in(own, axis_at), (blocks,), jnp.float32, least / len(cuts), top_value / len(cuts)))
        loudness = loudness * jnp.repeat(steps, shape[axis_at] // blocks).reshape([-1 if axis == axis_at else 1 for axis in range(len(shape))])
    return loudness


def gaussian_with(own_key, shape, spread, bound, cuts, heavy, held_as=jnp.bfloat16):
    values = spread * jax.random.normal(own_key, shape, jnp.float32)
    if cuts:
        values = values * level_of(own_key, shape, cuts, -0.22, 0.18)
    return jnp.clip(raised(values, jax.random.fold_in(own_key, 3), *heavy), -bound, bound).astype(held_as)


def setup_inputs(seed: int = 0) -> dict:
    keys = jax.random.split(jax.random.key(seed), 5)
    acts = gaussian_with(keys[0], (TOKENS, FF), 1.0, 6.0, ((0, 16), (1, 2)), (1, 0, 16, 2.0))
    grads = gaussian_with(keys[1], (TOKENS, D), 1.0, 6.0, ((0, 16), (1, 2)), (1, 0, 16, 2.0))
    in_factors = draw_in_factors(jax.random.fold_in(keys[4], 71), 0)
    out_factors = draw_out_factors(jax.random.fold_in(keys[4], 71), 0)
    return dict(acts=acts, grads=grads, in_factors=in_factors, out_factors=out_factors)


def reference(acts, grads, in_factors, out_factors):
    proj_in = jnp.dot(acts, in_factors, preferred_element_type=jnp.float32)
    proj_out = jnp.dot(grads, out_factors, preferred_element_type=jnp.float32)
    blocks_in = in_factors.astype(jnp.float32).reshape(FF, QUERIES, RANK)
    blocks_out = out_factors.astype(jnp.float32).reshape(D, QUERIES, RANK)
    gram_in = jnp.einsum('hqr,hqs->qrs', blocks_in, blocks_in)
    gram_out = jnp.einsum('hqr,hqs->qrs', blocks_out, blocks_out)
    qnorm = lax.optimization_barrier(jnp.sum(gram_in * gram_out, axis=(1, 2)))
    inverse = 1.0 / jnp.sqrt(qnorm + 1e-06)
    paired = (proj_in * proj_out).reshape(TOKENS, QUERIES, RANK).sum(axis=2)
    return paired * inverse[None, :]
```

```python
import functools
import math

import jax
import jax.numpy as jnp
from jax import lax
from jax.experimental import pallas as pl
from jax.experimental.pallas import tpu as pltpu
from jax.sharding import PartitionSpec as P

RANK = 32
WIDE = 256
LIGHT = pl.CostEstimate(flops=1, bytes_accessed=1, transcendentals=0)
ROOM = 24 << 20


def params():
    return pltpu.CompilerParams(vmem_limit_bytes=ROOM)


def cycle_of(first, second):
    if min(first, second) == 1:
        size = first * second
        order = list(range(0, size, 2)) + list(range(1, size, 2))[::-1]
        return [(i, 0) if second == 1 else (0, i) for i in order]
    if first % 2:
        return [(a, b) for b, a in cycle_of(second, first)] if second % 2 == 0 else [
            (a, b) for a in range(first) for b in range(second)]
    walk = []
    for a in range(first):
        inner = range(1, second)
        walk += [(a, b) for b in (inner if a % 2 == 0 else reversed(inner))]
    return walk + [(a, 0) for a in reversed(range(first))]


def ring_of(mesh):
    devices = list(mesh.devices[0])
    chips = {}
    for index, device in enumerate(devices):
        coords = getattr(device, "coords", None)
        key = tuple(coords) if coords is not None else (index // 2,)
        chips.setdefault(key, []).append(index)
    keys = list(chips)
    values = [sorted({k[i] for k in keys}) for i in range(len(keys[0]))]
    varying = [i for i in range(len(values)) if len(values[i]) > 1]
    if len(varying) == 2 and len(keys) == len(values[varying[0]]) * len(values[varying[1]]):
        one, two = sorted(varying, key=lambda i: -len(values[i]))
        at = {(values[one].index(k[one]), values[two].index(k[two])): k for k in keys}
        keys = [at[place] for place in cycle_of(len(values[one]), len(values[two]))]
    ring = [chips[k] for k in keys]
    assert all(pair[0] % 2 == 0 and pair[1] == pair[0] + 1 for pair in ring)
    return ring


def load_kernel(a_ref, b_ref, a_out, b_out, sem):
    first = pltpu.make_async_copy(a_ref, a_out, sem.at[0])
    second = pltpu.make_async_copy(b_ref, b_out, sem.at[1])
    first.start()
    second.start()
    first.wait()
    second.wait()


def load(a, b):
    return pl.pallas_call(
        load_kernel,
        in_specs=[pl.BlockSpec(memory_space=pl.ANY)] * 2,
        out_specs=[pl.BlockSpec(memory_space=pltpu.VMEM)] * 2,
        out_shape=[pltpu.VMEM(a.shape, a.dtype), pltpu.VMEM(b.shape, b.dtype)],
        scratch_shapes=[pltpu.SemaphoreType.DMA((2,))],
        compiler_params=params(),
        cost_estimate=LIGHT,
        name="load_factors",
    )(a, b)


def gram_kernel(step, a_ref, b_ref, out_ref, sums):
    columns = a_ref.shape[1]
    row = lax.broadcasted_iota(jnp.int32, (WIDE, WIDE), 0) // RANK
    col = lax.broadcasted_iota(jnp.int32, (WIDE, WIDE), 1) // RANK
    for index, ref in enumerate((a_ref, b_ref)):
        sums[...] = jnp.zeros_like(sums)

        @pl.loop(0, ref.shape[0] // step)
        def _(i, ref=ref):
            for start in range(0, columns, WIDE):
                block = ref[pl.ds(pl.multiple_of(i * step, step), step), start : start + WIDE]
                sums[:, start : start + WIDE] += lax.dot_general(
                    block, block, (((0,), (0,)), ((), ())), preferred_element_type=jnp.float32)

        for start in range(0, columns, WIDE):
            kept = jnp.where(row == col, sums[:, start : start + WIDE], 0.0)
            out_ref[index, :, start : start + WIDE] = kept.reshape(WIDE // RANK, RANK, WIDE).sum(axis=0)


def grams(a, b):
    columns = a.shape[1]
    step = math.gcd(a.shape[0], b.shape[0])
    return pl.pallas_call(
        functools.partial(gram_kernel, step),
        in_specs=[pl.BlockSpec(memory_space=pltpu.VMEM)] * 2,
        out_specs=pl.BlockSpec(memory_space=pltpu.VMEM),
        out_shape=jax.ShapeDtypeStruct((2, RANK, columns), jnp.float32),
        scratch_shapes=[pltpu.VMEM((WIDE, columns), jnp.float32)],
        compiler_params=params(),
        cost_estimate=LIGHT,
        name="grams",
    )(a, b)


def project_kernel(step, spans, *refs):
    count = sum(len(span[0]) for span in spans)
    tokens, factors, out_ref = refs[:count], refs[count : count + 2], refs[-1]
    i = pl.program_id(0)

    @pl.when(i == 0)
    def _():
        out_ref[...] = jnp.zeros_like(out_ref)

    first = 0
    taken = 0
    for widths, which, offset, steps in spans:
        held = tokens[taken : taken + len(widths)]

        @pl.when((i >= first) & (i < first + steps))
        def _(held=held, which=which, offset=offset, first=first):
            x = jnp.concatenate([h[...] for h in held], axis=0)
            at = pl.multiple_of((i - first) * step + offset, step)
            out_ref[which] += jnp.dot(x, factors[which][pl.ds(at, step), :], preferred_element_type=jnp.float32)

        first += steps
        taken += len(widths)


def project(groups, factors):
    sizes = [arrays[0].shape[1] for arrays, _, _ in groups] + [offset for _, _, offset in groups if offset]
    step = min(functools.reduce(math.gcd, sizes), 2048)
    spans, specs, operands, first = [], [], [], 0
    for arrays, which, offset in groups:
        steps = arrays[0].shape[1] // step
        spans.append((tuple(a.shape[0] for a in arrays), which, offset, steps))
        for a in arrays:
            specs.append(pl.BlockSpec(
                (a.shape[0], step), lambda i, first=first, steps=steps: (0, jnp.clip(i - first, 0, steps - 1))))
            operands.append(a)
        first += steps
    rows = sum(spans[0][0])
    columns = factors[0].shape[1]
    return pl.pallas_call(
        functools.partial(project_kernel, step, tuple(spans)),
        grid=(first,),
        in_specs=specs + [pl.BlockSpec(memory_space=pltpu.VMEM)] * 2,
        out_specs=pl.BlockSpec((2, rows, columns), lambda i: (0, 0, 0)),
        out_shape=jax.ShapeDtypeStruct((2, rows, columns), jnp.float32),
        compiler_params=params(),
        cost_estimate=LIGHT,
        name="project",
    )(*operands, *[pltpu.with_memory_space_constraint(f, pltpu.VMEM) for f in factors])


def scores_of(projected, gram, columns):
    queries = columns // RANK
    member = (lax.broadcasted_iota(jnp.int32, (columns, queries), 0) // RANK) == lax.broadcasted_iota(
        jnp.int32, (columns, queries), 1)
    member = member.astype(jnp.float32)

    def by_query(x):
        return jnp.dot(x, member, precision=lax.Precision.HIGHEST, preferred_element_type=jnp.float32)

    norms = jnp.broadcast_to((gram[0] * gram[1]).sum(axis=0, keepdims=True), (8, columns))
    inverse = 1.0 / jnp.sqrt(by_query(norms)[:1] + 1e-06)
    return by_query(projected[0] * projected[1]) * inverse


def total_of(refs):
    return sum(ref[...] for ref in refs[1:]) + refs[0][...]


def score_kernel(count, *refs):
    parts, grams_, out_ref = refs[:count], refs[count : 2 * count], refs[-1]
    out_ref[...] = scores_of(total_of(parts), total_of(grams_), out_ref.shape[1] * RANK)


def score(parts, gram_parts):
    rows, columns = parts[0].shape[1:]
    return pl.pallas_call(
        functools.partial(score_kernel, len(parts)),
        out_shape=jax.ShapeDtypeStruct((rows, columns // RANK), jnp.float32),
        compiler_params=params(),
        cost_estimate=LIGHT,
        name="score",
    )(*parts, *gram_parts)


def looked_up(table, index):
    return sum(jnp.where(index == i, value, 0) for i, value in enumerate(table))


def last_kernel(count, distances, place, tokens, at_ref, *refs):
    parts, grams_ = refs[:count], refs[count : 2 * count]
    earlier, out_ref, held = refs[2 * count : -2], refs[-2], refs[-1]
    columns = parts[0].shape[2]
    chips = len(place)
    known = [*(ref[...] for ref in earlier)]
    if parts:
        known.append(scores_of(total_of(parts), total_of(grams_), columns))
    for group, result in zip(distances, known):
        for c in range(2):
            for j, distance in enumerate(group):
                begin = (c * len(group) + j) * tokens
                held[distance % chips, c] = result[begin : begin + tokens]
    core, side = at_ref[0], at_ref[1]
    here = looked_up(place, core // 2)
    own = core % 2
    share = out_ref.shape[0] // (2 * tokens)
    for j in range(share):
        there = looked_up(place, side * share + j)
        distance = there - here
        distance = jnp.where(distance < 0, distance + chips, distance)
        for c in range(2):
            out_ref[(2 * j + c) * tokens : (2 * j + c + 1) * tokens, :] = held[distance, (own + c) % 2]


def last(parts, gram_parts, earlier, distances, place, tokens, share, at):
    queries = earlier[0].shape[1]
    return pl.pallas_call(
        functools.partial(last_kernel, len(parts), distances, place, tokens),
        in_specs=[pl.BlockSpec(memory_space=pltpu.SMEM)]
        + [pl.BlockSpec(memory_space=pltpu.VMEM)] * (len(parts) + len(gram_parts) + len(earlier)),
        out_specs=pl.BlockSpec(memory_space=pltpu.VMEM),
        out_shape=jax.ShapeDtypeStruct((share, queries), jnp.float32),
        scratch_shapes=[pltpu.VMEM((len(place), 2, tokens, queries), jnp.float32)],
        compiler_params=params(),
        cost_estimate=LIGHT,
        name="last_scores",
    )(at, *parts, *gram_parts, *earlier)


def solution(mesh):
    rows = mesh.shape["rows"]
    query = mesh.shape["query"]
    ring = ring_of(mesh)
    chips = len(ring)
    forward = [(a, b) for i in range(chips) for a, b in zip(ring[i], ring[(i + 1) % chips])]
    backward = [(b, a) for a, b in forward]
    mates = [(pair[i], pair[1 - i]) for pair in ring for i in range(2)]
    place = [0] * chips
    for i, pair in enumerate(ring):
        place[pair[0] // 2] = i
    place = tuple(place)

    def across(x):
        if rows == 2:
            return [x, lax.ppermute(x, "rows", [(0, 1), (1, 0)])]
        return [lax.psum(x, "rows")]

    def mate(x):
        return lax.ppermute(x, "query", mates)

    def ahead(x):
        return lax.ppermute(x, "query", forward)

    def behind(x):
        return lax.ppermute(x, "query", backward)

    def tied(*trees):
        return lax.optimization_barrier(trees)

    def local(acts, grads, in_factors, out_factors):
        tokens, width = acts.shape
        cut = (width + grads.shape[1]) // 2 // 128 * 128
        at = jnp.stack([lax.axis_index("query"), lax.axis_index("rows")]).astype(jnp.int32)
        full_hops = (chips - 1) // 2

        flying = ahead(acts), behind(acts), ahead(grads), behind(grads)
        a, g = mate(acts), mate(grads)
        factors = load(in_factors, out_factors)
        gram = grams(*factors)
        projected = project([([acts, a], 0, 0), ([grads, g], 1, 0)], factors)
        flying, projected, gram = tied(flying, projected, gram)
        gram_parts = across(gram)
        groups = [(0,)]
        done = []
        waiting = []
        for hop in range(1, full_hops + 1):
            a_f, a_b, g_f, g_b = flying
            if hop < full_hops:
                flying = ahead(a_f), behind(a_b), ahead(g_f), behind(g_b)
            elif chips % 2 == 0:
                flying = ahead(a_f[:, :cut]), behind(a_b[:, cut:]), behind(g_b)
            swapped = [mate(x) for x in (a_f, a_b, g_f, g_b)]
            parts = across(projected)
            if waiting:
                done.append(score(waiting, gram_parts))
            projected = project(
                [([a_f, a_b, swapped[0], swapped[1]], 0, 0), ([g_f, g_b, swapped[2], swapped[3]], 1, 0)], factors)
            groups.append((-hop, hop))
            flying, projected, waiting, gram_parts, done = tied(flying, projected, parts, gram_parts, done)
        parts = across(projected)
        done.append(score(waiting, gram_parts))
        tail = []
        if chips % 2 == 0:
            a_f, a_b, g_b = flying
            swapped = [mate(x) for x in flying]
            projected = project(
                [([g_b, swapped[2]], 1, 0), ([a_f, swapped[0]], 0, 0), ([a_b, swapped[1]], 0, cut)], factors)
            tail = across(projected)
            groups.append((chips // 2,))
        done.append(score(parts, gram_parts))
        return last(tail, gram_parts if tail else [], done, groups, place, tokens, query * tokens // rows, at)

    return jax.shard_map(
        local,
        mesh=mesh,
        in_specs=(P("query", "rows"), P("query", "rows"), P("rows", "query"), P("rows", "query")),
        out_specs=P("rows", "query"),
        check_vma=False,
    )
```

```python
import functools
import math

import jax
import jax.numpy as jnp
from jax import lax
from jax.experimental import pallas as pl
from jax.experimental.pallas import tpu as pltpu
from jax.sharding import PartitionSpec as P

RANK = 32
WIDE = 256
LIGHT = pl.CostEstimate(flops=1, bytes_accessed=1, transcendentals=0)
ROOM = 16 << 20


def params():
    return pltpu.CompilerParams(vmem_limit_bytes=ROOM)


def in_hbm(x):
    return pltpu.with_memory_space_constraint(x, pltpu.HBM)


def in_vmem(x):
    return pltpu.with_memory_space_constraint(x, pltpu.VMEM)


def cycle_of(first, second):
    if min(first, second) == 1:
        size = first * second
        order = list(range(0, size, 2)) + list(range(1, size, 2))[::-1]
        return [(i, 0) if second == 1 else (0, i) for i in order]
    if first % 2:
        return [(a, b) for b, a in cycle_of(second, first)] if second % 2 == 0 else [
            (a, b) for a in range(first) for b in range(second)]
    walk = []
    for a in range(first):
        inner = range(1, second)
        walk += [(a, b) for b in (inner if a % 2 == 0 else reversed(inner))]
    return walk + [(a, 0) for a in reversed(range(first))]


def ring_of(mesh):
    devices = list(mesh.devices[0])
    chips = {}
    for index, device in enumerate(devices):
        coords = getattr(device, "coords", None)
        key = tuple(coords) if coords is not None else (index // 2,)
        chips.setdefault(key, []).append(index)
    keys = list(chips)
    values = [sorted({k[i] for k in keys}) for i in range(len(keys[0]))]
    varying = [i for i in range(len(values)) if len(values[i]) > 1]
    if len(varying) == 2 and len(keys) == len(values[varying[0]]) * len(values[varying[1]]):
        one, two = sorted(varying, key=lambda i: -len(values[i]))
        at = {(values[one].index(k[one]), values[two].index(k[two])): k for k in keys}
        keys = [at[place] for place in cycle_of(len(values[one]), len(values[two]))]
    ring = [chips[k] for k in keys]
    assert all(pair[0] % 2 == 0 and pair[1] == pair[0] + 1 for pair in ring)
    return ring


def load_kernel(a_ref, b_ref, a_out, b_out, sem):
    first = pltpu.make_async_copy(a_ref, a_out, sem.at[0])
    second = pltpu.make_async_copy(b_ref, b_out, sem.at[1])
    first.start()
    second.start()
    first.wait()
    second.wait()


def load(a, b):
    return pl.pallas_call(
        load_kernel,
        in_specs=[pl.BlockSpec(memory_space=pl.ANY)] * 2,
        out_specs=[pl.BlockSpec(memory_space=pltpu.VMEM)] * 2,
        out_shape=[pltpu.VMEM(a.shape, a.dtype), pltpu.VMEM(b.shape, b.dtype)],
        scratch_shapes=[pltpu.SemaphoreType.DMA((2,))],
        compiler_params=params(),
        cost_estimate=LIGHT,
        name="load_factors",
    )(in_hbm(a), in_hbm(b))


def join_kernel(a_ref, b_ref, out_ref, sem):
    width = a_ref.shape[1]
    first = pltpu.make_async_copy(a_ref, out_ref.at[:, :width], sem.at[0])
    second = pltpu.make_async_copy(b_ref, out_ref.at[:, width:], sem.at[1])
    first.start()
    second.start()
    first.wait()
    second.wait()


def joined(a, b):
    return pl.pallas_call(
        join_kernel,
        in_specs=[pl.BlockSpec(memory_space=pl.ANY)] * 2,
        out_specs=pl.BlockSpec(memory_space=pl.ANY),
        out_shape=jax.ShapeDtypeStruct((a.shape[0], a.shape[1] + b.shape[1]), a.dtype),
        scratch_shapes=[pltpu.SemaphoreType.DMA((2,))],
        compiler_params=params(),
        cost_estimate=LIGHT,
        name="join",
    )(in_hbm(a), in_hbm(b))


def pack_kernel(count, parts, step, *refs):
    arrays, outs = refs[:count], refs[count:]
    i = pl.program_id(0)
    for out, (first, steps) in zip(outs, parts):

        @pl.when((i >= first) & (i < first + steps))
        def _(out=out):
            out[...] = jnp.concatenate([x[...] for x in arrays], axis=0)


def packed(arrays, bounds, step):
    rows = sum(a.shape[0] for a in arrays)
    parts = tuple((lo // step, (hi - lo) // step) for lo, hi in zip(bounds, bounds[1:]))
    return pl.pallas_call(
        functools.partial(pack_kernel, len(arrays), parts, step),
        grid=(bounds[-1] // step,),
        in_specs=[pl.BlockSpec((a.shape[0], step), lambda i: (0, i)) for a in arrays],
        out_specs=[
            pl.BlockSpec((rows, step), lambda i, first=first, steps=steps: (0, jnp.clip(i - first, 0, steps - 1)))
            for first, steps in parts],
        out_shape=[jax.ShapeDtypeStruct((rows, hi - lo), arrays[0].dtype) for lo, hi in zip(bounds, bounds[1:])],
        compiler_params=params(),
        cost_estimate=LIGHT,
        name="pack",
    )(*arrays)


def cut_kernel(a_ref, b_ref, a_out, b_out, sem):
    width = a_out.shape[1]
    first = pltpu.make_async_copy(a_ref.at[:, :width], a_out, sem.at[0])
    second = pltpu.make_async_copy(b_ref.at[:, width:], b_out, sem.at[1])
    first.start()
    second.start()
    first.wait()
    second.wait()


def cut_halves(a, b, middle):
    return pl.pallas_call(
        cut_kernel,
        in_specs=[pl.BlockSpec(memory_space=pl.ANY)] * 2,
        out_specs=[pl.BlockSpec(memory_space=pl.ANY)] * 2,
        out_shape=[
            jax.ShapeDtypeStruct((a.shape[0], middle), a.dtype),
            jax.ShapeDtypeStruct((b.shape[0], b.shape[1] - middle), b.dtype)],
        scratch_shapes=[pltpu.SemaphoreType.DMA((2,))],
        compiler_params=params(),
        cost_estimate=LIGHT,
        name="cut",
    )(a, b)


def gram_kernel(step, a_ref, b_ref, out_ref, sums):
    columns = a_ref.shape[1]
    row = lax.broadcasted_iota(jnp.int32, (WIDE, WIDE), 0) // RANK
    col = lax.broadcasted_iota(jnp.int32, (WIDE, WIDE), 1) // RANK
    for index, ref in enumerate((a_ref, b_ref)):
        sums[...] = jnp.zeros_like(sums)

        @pl.loop(0, ref.shape[0] // step)
        def _(i, ref=ref):
            for start in range(0, columns, WIDE):
                block = ref[pl.ds(pl.multiple_of(i * step, step), step), start : start + WIDE]
                sums[:, start : start + WIDE] += lax.dot_general(
                    block, block, (((0,), (0,)), ((), ())), preferred_element_type=jnp.float32)

        for start in range(0, columns, WIDE):
            kept = jnp.where(row == col, sums[:, start : start + WIDE], 0.0)
            out_ref[index, :, start : start + WIDE] = kept.reshape(WIDE // RANK, RANK, WIDE).sum(axis=0)


def grams(a, b):
    columns = a.shape[1]
    step = math.gcd(a.shape[0], b.shape[0])
    return pl.pallas_call(
        functools.partial(gram_kernel, step),
        in_specs=[pl.BlockSpec(memory_space=pltpu.VMEM)] * 2,
        out_specs=pl.BlockSpec(memory_space=pltpu.VMEM),
        out_shape=jax.ShapeDtypeStruct((2, RANK, columns), jnp.float32),
        scratch_shapes=[pltpu.VMEM((WIDE, columns), jnp.float32)],
        compiler_params=params(),
        cost_estimate=LIGHT,
        name="grams",
    )(a, b)


def chunk_of(*sizes):
    step = functools.reduce(math.gcd, sizes)
    for least in (1024, 512, 256, 128):
        if step % least == 0:
            return least
    return step


def project_kernel(step, spans, count, split, side_ref, *refs):
    outs, sums = refs[count + 2 : -1], refs[-1]
    factors = refs[count : count + 2]
    i = pl.program_id(0)

    @pl.when(i == 0)
    def _():
        sums[...] = jnp.zeros_like(sums)

    for held, first, steps, which, offset in spans:

        @pl.when((i >= first) & (i < first + steps))
        def _(held=held, which=which, offset=offset, first=first):
            x = jnp.concatenate([refs[h][...] for h in held], axis=0)
            at = pl.multiple_of((i - first) * step + offset, step)
            sums[which if split else 0] += jnp.dot(
                x, factors[which][pl.ds(at, step), :], preferred_element_type=jnp.float32)

    @pl.when(i == pl.num_programs(0) - 1)
    def _():
        if split:
            half = sums.shape[1] // 2
            side = side_ref[0]
            for out, which in zip(outs, (side, 1 - side)):
                out[...] = sums[:, pl.ds(pl.multiple_of(which * half, 8), half), :]
        else:
            outs[0][...] = sums[0]


def project(groups, factors, side, split, step):
    specs, operands, spans, first = [], [], [], 0
    for arrays, group in groups:
        held = tuple(range(len(operands), len(operands) + len(arrays)))
        low = min(begin for begin, _, _, _ in group) // step
        high = max(begin + width for begin, width, _, _ in group) // step
        for array, base in arrays:
            specs.append(pl.BlockSpec(
                (array.shape[0], step),
                lambda i, first=first, low=low, high=high, base=base // step:
                    (0, base + jnp.clip(i - first + low, low, high - 1))))
            operands.append(array)
        for begin, width, which, offset in group:
            spans.append((held, first + begin // step - low, width // step, which, offset))
        first += high - low
    rows, columns = sum(a.shape[0] for a, _ in groups[0][0]), factors[0].shape[1]
    shape = (2, rows // 2, columns) if split else (rows, columns)
    outs = 2 if split else 1
    return pl.pallas_call(
        functools.partial(project_kernel, step, tuple(spans), len(operands), split),
        grid=(first,),
        in_specs=[pl.BlockSpec(memory_space=pltpu.SMEM)] + specs + [pl.BlockSpec(memory_space=pltpu.VMEM)] * 2,
        out_specs=[pl.BlockSpec(shape, lambda i: (0,) * len(shape))] * outs,
        out_shape=[jax.ShapeDtypeStruct(shape, jnp.float32)] * outs,
        scratch_shapes=[pltpu.VMEM((outs, rows, columns), jnp.float32)],
        compiler_params=params(),
        cost_estimate=LIGHT,
        name="project",
    )(side, *operands, *[in_vmem(f) for f in factors])


def project_last_kernel(pieces, *refs):
    count = sum(arrays for arrays, _ in pieces)
    tokens, factors, out_ref = refs[:count], refs[count : count + 2], refs[-1]
    out_ref[...] = jnp.zeros_like(out_ref)
    taken = 0
    for arrays, spans in pieces:
        held = tokens[taken : taken + arrays]
        taken += arrays
        for begin, width, which, offset in spans:
            step = chunk_of(width)

            @pl.loop(0, width // step)
            def _(i, held=held, begin=begin, which=which, offset=offset, step=step):
                at = pl.ds(pl.multiple_of(i * step + begin, 128), step)
                x = jnp.concatenate([h[:, at] for h in held], axis=0)
                w = factors[which][pl.ds(pl.multiple_of(i * step + offset, 128), step), :]
                out_ref[...] += jnp.dot(x, w, preferred_element_type=jnp.float32)


def project_last(groups, factors):
    pieces = tuple((len(arrays), tuple(spans)) for arrays, spans in groups)
    operands = [a for arrays, _ in groups for a in arrays]
    rows, columns = sum(a.shape[0] for a in groups[0][0]), factors[0].shape[1]
    given = [in_vmem(x) for x in (*operands, *factors)]
    return pl.pallas_call(
        functools.partial(project_last_kernel, pieces),
        in_specs=[pl.BlockSpec(memory_space=pltpu.VMEM)] * len(given),
        out_specs=pl.BlockSpec(memory_space=pltpu.VMEM),
        out_shape=jax.ShapeDtypeStruct((rows, columns), jnp.float32),
        compiler_params=params(),
        cost_estimate=LIGHT,
        name="project_last",
    )(*given)


def scores_of(projected, gram, columns):
    queries = columns // RANK
    member = (lax.broadcasted_iota(jnp.int32, (columns, queries), 0) // RANK) == lax.broadcasted_iota(
        jnp.int32, (columns, queries), 1)
    member = member.astype(jnp.float32)

    def by_query(x):
        return jnp.dot(x, member, precision=lax.Precision.HIGHEST, preferred_element_type=jnp.float32)

    norms = jnp.broadcast_to((gram[0] * gram[1]).sum(axis=0, keepdims=True), (8, columns))
    inverse = 1.0 / jnp.sqrt(by_query(norms)[:1] + 1e-06)
    return by_query(projected[0] * projected[1]) * inverse


def total_of(refs):
    return sum(ref[...] for ref in refs[1:]) + refs[0][...]


def score_kernel(counts, grams_count, *refs):
    grams_, out_ref = refs[-1 - grams_count : -1], refs[-1]
    columns = grams_[0].shape[2]
    taken, first = 0, 0
    for count in counts:
        parts = refs[taken : taken + count]
        taken += count
        rows = parts[0].shape[1]
        out_ref[first : first + rows] = scores_of(total_of(parts), total_of(grams_), columns)
        first += rows


def score(groups, gram_parts):
    columns = gram_parts[0].shape[2]
    return pl.pallas_call(
        functools.partial(score_kernel, tuple(len(parts) for parts in groups), len(gram_parts)),
        out_shape=jax.ShapeDtypeStruct((sum(parts[0].shape[1] for parts in groups), columns // RANK), jnp.float32),
        compiler_params=params(),
        cost_estimate=LIGHT,
        name="score",
    )(*[p for parts in groups for p in parts], *gram_parts)


def looked_up(table, index):
    return sum(jnp.where(index == i, value, 0) for i, value in enumerate(table))


def last_kernel(count, distances, place, tokens, at_ref, *refs):
    parts = refs[: 2 * count]
    grams_ = refs[2 * count : 3 * count]
    earlier, out_ref, held = refs[3 * count : -2], refs[-2], refs[-1]
    chips = len(place)
    core, side, keeper = at_ref[0], at_ref[1], at_ref[2]
    for groups, mine, other in zip(distances, earlier[0::2], earlier[1::2]):
        for j, distance in enumerate(groups):
            held[distance % chips, keeper] = mine[j * tokens : (j + 1) * tokens]
            held[distance % chips, 1 - keeper] = other[j * tokens : (j + 1) * tokens]
    if count:
        projected = [total_of(parts[:count]), total_of(parts[count:])]
        result = scores_of(projected, total_of(grams_), projected[0].shape[1])
        for c in range(2):
            held[chips // 2, c] = result[c * tokens : (c + 1) * tokens]
    here = looked_up(place, core // 2)
    own = core % 2
    share = out_ref.shape[0] // (2 * tokens)
    for j in range(share):
        there = looked_up(place, side * share + j)
        distance = there - here
        distance = jnp.where(distance < 0, distance + chips, distance)
        for c in range(2):
            out_ref[(2 * j + c) * tokens : (2 * j + c + 1) * tokens, :] = held[distance, (own + c) % 2]


def last(first, second, gram_parts, earlier, distances, place, tokens, share, at):
    queries = earlier[0].shape[1]
    return pl.pallas_call(
        functools.partial(last_kernel, len(first), distances, place, tokens),
        in_specs=[pl.BlockSpec(memory_space=pltpu.SMEM)]
        + [pl.BlockSpec(memory_space=pltpu.VMEM)] * (3 * len(first) + len(earlier)),
        out_specs=pl.BlockSpec(memory_space=pltpu.VMEM),
        out_shape=jax.ShapeDtypeStruct((share, queries), jnp.float32),
        scratch_shapes=[pltpu.VMEM((len(place), 2, tokens, queries), jnp.float32)],
        compiler_params=params(),
        cost_estimate=LIGHT,
        name="last_scores",
    )(at, *first, *second, *gram_parts[: len(first)], *earlier)


def within(spans, low, high):
    kept = []
    for begin, width, which, offset in spans:
        a, b = max(begin, low), min(begin + width, high)
        if a < b:
            kept.append((a - low, b - a, which, offset + a - begin))
    return kept


def solution(mesh):
    rows = mesh.shape["rows"]
    query = mesh.shape["query"]
    ring = ring_of(mesh)
    chips = len(ring)
    forward = [(a, b) for i in range(chips) for a, b in zip(ring[i], ring[(i + 1) % chips])]
    backward = [(b, a) for a, b in forward]
    mates = [(pair[i], pair[1 - i]) for pair in ring for i in range(2)]
    place = [0] * chips
    for i, pair in enumerate(ring):
        place[pair[0] // 2] = i
    place = tuple(place)

    def swap_rows(x):
        return lax.ppermute(x, "rows", [(0, 1), (1, 0)])

    def across(x):
        return [x, swap_rows(x)] if rows == 2 else [lax.psum(x, "rows")]

    def mate(xs):
        return [lax.ppermute(x, "query", mates) for x in xs]

    def ahead(x):
        return lax.ppermute(x, "query", forward)

    def behind(x):
        return lax.ppermute(x, "query", backward)

    def both(pair):
        return [ahead(pair[0]), behind(pair[1])]

    def tied(*trees):
        return lax.optimization_barrier(trees)

    def local(acts, grads, in_factors, out_factors):
        tokens, width = acts.shape
        depth = grads.shape[1]
        total = width + depth
        middle = total // 2 // 128 * 128
        span = [(0, depth, 1, 0), (depth, width, 0, 0)]
        query_at, row_at = lax.axis_index("query"), lax.axis_index("rows")
        keeper = row_at if rows == 2 else jnp.zeros_like(row_at)
        at = jnp.stack([query_at, row_at, keeper]).astype(jnp.int32)
        side = keeper.astype(jnp.int32).reshape(1)
        full_hops = (chips - 1) // 2

        step = math.gcd(width, depth)
        while step > 2048 and step % 2 == 0:
            step //= 2
        bounds = [total * i // 3 // step * step for i in range(4)]

        def mates_of(held):
            return mate(packed(held, bounds, step))

        def projected(held, swapped):
            groups = [
                ([(x, lo) for x in held] + [(part, 0)], within(span, lo, hi))
                for lo, hi, part in zip(bounds, bounds[1:], swapped)]
            return project(groups, factors, side, True, step)

        def exchanged(kept, sent):
            if rows == 2:
                return [[kept, swap_rows(sent)]]
            return [[x] for x in lax.psum((kept, sent), "rows")]

        def scored(held):
            return [score(list(groups), gram_parts) for groups in zip(*held)]

        at, side, acts, grads, in_factors, out_factors = tied(at, side, acts, grads, in_factors, out_factors)
        own = joined(grads, acts)
        fly = [ahead(own), behind(own)]
        swapped = mates_of([own])
        factors = load(in_factors, out_factors)
        gram = grams(*factors)
        kept, sent = projected([own], swapped)
        fly, gram, kept, sent = tied(fly, gram, kept, sent)
        own_sums = (kept, sent)
        distances, waiting = [0], []
        for hop in range(1, full_hops + 1):
            held = fly
            final = hop == full_hops
            if not final:
                fly = [ahead(held[0]), behind(held[1])]
            elif chips % 2 == 0:
                fly = cut_halves(*held, middle)
                fly = [ahead(fly[0]), behind(fly[1])]
            swapped = mates_of(held)
            kept, sent = projected(held, swapped)
            kept, sent, waiting = tied(kept, sent, waiting)
            halves = exchanged(kept, sent)
            if hop == 1:
                waiting.append(exchanged(*own_sums))
                gram_parts = across(gram)
            if not final:
                distances += [-hop, hop]
                waiting.append(halves)
            fly, halves, waiting, gram_parts = tied(fly, halves, waiting, gram_parts)
        mine, *other = scored(waiting)
        result, *second_half = scored([halves])
        if rows == 2:
            other, second_half = [swap_rows(mine)], [swap_rows(result)]
        first, second = [], []
        if chips % 2 == 0:
            parts = mate(fly)
            fly, parts = tied(fly, parts)
            low, high = within(span, 0, middle), within(span, middle, total)
            out = project_last([([fly[0], parts[0]], [s for s in low if s[2]])], factors)
            first = across(out)
            fly, parts, out, other, second_half = tied(fly, parts, out, other, second_half)
            second = across(project_last([
                ([fly[0], parts[0]], [s for s in low if not s[2]]), ([fly[1], parts[1]], high)], factors))
        return last(
            first, second, gram_parts, [mine, *other, result, *second_half],
            (tuple(distances), (-full_hops, full_hops)), place, tokens, query * tokens // rows, at)

    return jax.shard_map(
        local,
        mesh=mesh,
        in_specs=(P("query", "rows"), P("query", "rows"), P("rows", "query"), P("rows", "query")),
        out_specs=P("rows", "query"),
        check_vma=False,
    )
```

```python
import functools
import math

import jax
import jax.numpy as jnp
from jax import lax
from jax.experimental import pallas as pl
from jax.experimental.pallas import tpu as pltpu
from jax.sharding import PartitionSpec as P

RANK = 32
WIDE = 256
LIGHT = pl.CostEstimate(flops=1, bytes_accessed=1, transcendentals=0)
ROOM = 16 << 20


def params():
    return pltpu.CompilerParams(vmem_limit_bytes=ROOM)


def in_hbm(x):
    return pltpu.with_memory_space_constraint(x, pltpu.HBM)


def in_vmem(x):
    return pltpu.with_memory_space_constraint(x, pltpu.VMEM)


def cycle_of(first, second):
    if min(first, second) == 1:
        size = first * second
        order = list(range(0, size, 2)) + list(range(1, size, 2))[::-1]
        return [(i, 0) if second == 1 else (0, i) for i in order]
    if first % 2:
        return [(a, b) for b, a in cycle_of(second, first)] if second % 2 == 0 else [
            (a, b) for a in range(first) for b in range(second)]
    walk = []
    for a in range(first):
        inner = range(1, second)
        walk += [(a, b) for b in (inner if a % 2 == 0 else reversed(inner))]
    return walk + [(a, 0) for a in reversed(range(first))]


def ring_of(mesh):
    devices = list(mesh.devices[0])
    chips = {}
    for index, device in enumerate(devices):
        coords = getattr(device, "coords", None)
        key = tuple(coords) if coords is not None else (index // 2,)
        chips.setdefault(key, []).append(index)
    keys = list(chips)
    values = [sorted({k[i] for k in keys}) for i in range(len(keys[0]))]
    varying = [i for i in range(len(values)) if len(values[i]) > 1]
    if len(varying) == 2 and len(keys) == len(values[varying[0]]) * len(values[varying[1]]):
        one, two = sorted(varying, key=lambda i: -len(values[i]))
        at = {(values[one].index(k[one]), values[two].index(k[two])): k for k in keys}
        keys = [at[place] for place in cycle_of(len(values[one]), len(values[two]))]
    ring = [chips[k] for k in keys]
    assert all(pair[0] % 2 == 0 and pair[1] == pair[0] + 1 for pair in ring)
    return ring


def load_kernel(a_ref, b_ref, a_out, b_out, sem):
    first = pltpu.make_async_copy(a_ref, a_out, sem.at[0])
    second = pltpu.make_async_copy(b_ref, b_out, sem.at[1])
    first.start()
    second.start()
    first.wait()
    second.wait()


def load(a, b):
    return pl.pallas_call(
        load_kernel,
        in_specs=[pl.BlockSpec(memory_space=pl.ANY)] * 2,
        out_specs=[pl.BlockSpec(memory_space=pltpu.VMEM)] * 2,
        out_shape=[pltpu.VMEM(a.shape, a.dtype), pltpu.VMEM(b.shape, b.dtype)],
        scratch_shapes=[pltpu.SemaphoreType.DMA((2,))],
        compiler_params=params(),
        cost_estimate=LIGHT,
        name="load_factors",
    )(in_hbm(a), in_hbm(b))


def join_kernel(a_ref, b_ref, out_ref, sem):
    width = a_ref.shape[1]
    first = pltpu.make_async_copy(a_ref, out_ref.at[:, :width], sem.at[0])
    second = pltpu.make_async_copy(b_ref, out_ref.at[:, width:], sem.at[1])
    first.start()
    second.start()
    first.wait()
    second.wait()


def joined(a, b):
    return pl.pallas_call(
        join_kernel,
        in_specs=[pl.BlockSpec(memory_space=pl.ANY)] * 2,
        out_specs=pl.BlockSpec(memory_space=pl.ANY),
        out_shape=jax.ShapeDtypeStruct((a.shape[0], a.shape[1] + b.shape[1]), a.dtype),
        scratch_shapes=[pltpu.SemaphoreType.DMA((2,))],
        compiler_params=params(),
        cost_estimate=LIGHT,
        name="join",
    )(in_hbm(a), in_hbm(b))


def pack_kernel(count, parts, step, *refs):
    arrays, outs = refs[:count], refs[count:]
    i = pl.program_id(0)
    for out, (first, steps) in zip(outs, parts):

        @pl.when((i >= first) & (i < first + steps))
        def _(out=out):
            out[...] = jnp.concatenate([x[...] for x in arrays], axis=0)


def packed(arrays, bounds, step):
    rows = sum(a.shape[0] for a in arrays)
    parts = tuple((lo // step, (hi - lo) // step) for lo, hi in zip(bounds, bounds[1:]))
    return pl.pallas_call(
        functools.partial(pack_kernel, len(arrays), parts, step),
        grid=(bounds[-1] // step,),
        in_specs=[pl.BlockSpec((a.shape[0], step), lambda i: (0, i)) for a in arrays],
        out_specs=[
            pl.BlockSpec((rows, step), lambda i, first=first, steps=steps: (0, jnp.clip(i - first, 0, steps - 1)))
            for first, steps in parts],
        out_shape=[jax.ShapeDtypeStruct((rows, hi - lo), arrays[0].dtype) for lo, hi in zip(bounds, bounds[1:])],
        compiler_params=params(),
        cost_estimate=LIGHT,
        name="pack",
    )(*arrays)


def cut_kernel(ranges, a_ref, b_ref, *refs):
    outs, sem = refs[:-1], refs[-1]
    copies = [
        pltpu.make_async_copy((a_ref, b_ref)[which].at[:, lo:hi], out, sem.at[index])
        for index, (out, (which, lo, hi)) in enumerate(zip(outs, ranges))]
    for copy in copies:
        copy.start()
    for copy in copies:
        copy.wait()


def column_ranges(a, b, ranges):
    return pl.pallas_call(
        functools.partial(cut_kernel, tuple(ranges)),
        in_specs=[pl.BlockSpec(memory_space=pl.ANY)] * 2,
        out_specs=[pl.BlockSpec(memory_space=pl.ANY)] * len(ranges),
        out_shape=[jax.ShapeDtypeStruct((a.shape[0], hi - lo), a.dtype) for _, lo, hi in ranges],
        scratch_shapes=[pltpu.SemaphoreType.DMA((len(ranges),))],
        compiler_params=params(),
        cost_estimate=LIGHT,
        name="cut",
    )(a, b)


def gram_kernel(step, a_ref, b_ref, out_ref, sums):
    columns = a_ref.shape[1]
    row = lax.broadcasted_iota(jnp.int32, (WIDE, WIDE), 0) // RANK
    col = lax.broadcasted_iota(jnp.int32, (WIDE, WIDE), 1) // RANK
    for index, ref in enumerate((a_ref, b_ref)):
        sums[...] = jnp.zeros_like(sums)

        @pl.loop(0, ref.shape[0] // step)
        def _(i, ref=ref):
            for start in range(0, columns, WIDE):
                block = ref[pl.ds(pl.multiple_of(i * step, step), step), start : start + WIDE]
                sums[:, start : start + WIDE] += lax.dot_general(
                    block, block, (((0,), (0,)), ((), ())), preferred_element_type=jnp.float32)

        for start in range(0, columns, WIDE):
            kept = jnp.where(row == col, sums[:, start : start + WIDE], 0.0)
            out_ref[index, :, start : start + WIDE] = kept.reshape(WIDE // RANK, RANK, WIDE).sum(axis=0)


def grams(a, b):
    columns = a.shape[1]
    step = math.gcd(a.shape[0], b.shape[0])
    return pl.pallas_call(
        functools.partial(gram_kernel, step),
        in_specs=[pl.BlockSpec(memory_space=pltpu.VMEM)] * 2,
        out_specs=pl.BlockSpec(memory_space=pltpu.VMEM),
        out_shape=jax.ShapeDtypeStruct((2, RANK, columns), jnp.float32),
        scratch_shapes=[pltpu.VMEM((WIDE, columns), jnp.float32)],
        compiler_params=params(),
        cost_estimate=LIGHT,
        name="grams",
    )(a, b)


def chunk_of(*sizes):
    step = functools.reduce(math.gcd, sizes)
    for least in (1024, 512, 256, 128):
        if step % least == 0:
            return least
    return step


def project_kernel(step, spans, count, *refs):
    factors, out_ref = refs[count : count + 2], refs[-1]
    i = pl.program_id(0)

    @pl.when(i == 0)
    def _():
        out_ref[...] = jnp.zeros_like(out_ref)

    for held, first, steps, which, offset in spans:

        @pl.when((i >= first) & (i < first + steps))
        def _(held=held, which=which, offset=offset, first=first):
            x = jnp.concatenate([refs[h][...] for h in held], axis=0)
            at = pl.multiple_of((i - first) * step + offset, step)
            out_ref[...] += jnp.dot(x, factors[which][pl.ds(at, step), :], preferred_element_type=jnp.float32)


def project(groups, factors, step):
    specs, operands, spans, first = [], [], [], 0
    for arrays, group in groups:
        held = tuple(range(len(operands), len(operands) + len(arrays)))
        low = min(begin for begin, _, _, _ in group) // step
        high = max(begin + width for begin, width, _, _ in group) // step
        for array, base in arrays:
            specs.append(pl.BlockSpec(
                (array.shape[0], step),
                lambda i, first=first, low=low, high=high, base=base // step:
                    (0, base + jnp.clip(i - first + low, low, high - 1))))
            operands.append(array)
        for begin, width, which, offset in group:
            spans.append((held, first + begin // step - low, width // step, which, offset))
        first += high - low
    shape = (sum(a.shape[0] for a, _ in groups[0][0]), factors[0].shape[1])
    return pl.pallas_call(
        functools.partial(project_kernel, step, tuple(spans), len(operands)),
        grid=(first,),
        in_specs=specs + [pl.BlockSpec(memory_space=pltpu.VMEM)] * 2,
        out_specs=pl.BlockSpec(shape, lambda i: (0, 0)),
        out_shape=jax.ShapeDtypeStruct(shape, jnp.float32),
        compiler_params=params(),
        cost_estimate=LIGHT,
        name="project",
    )(*operands, *[in_vmem(f) for f in factors])


def by_query(x):
    columns = x.shape[1]
    queries = columns // RANK
    member = (lax.broadcasted_iota(jnp.int32, (columns, queries), 0) // RANK) == lax.broadcasted_iota(
        jnp.int32, (columns, queries), 1)
    return jnp.dot(
        x, member.astype(jnp.float32), precision=lax.Precision.HIGHEST, preferred_element_type=jnp.float32)


def total_of(refs):
    return sum(ref[...] for ref in refs[1:]) + refs[0][...]


def project_last_kernel(pieces, more, pairs, *refs):
    count = sum(arrays for arrays, _ in pieces)
    tokens, factors, out_ref, sums = refs[:count], refs[count : count + 2], refs[-2], refs[-1]
    sums[...] = refs[count + 2][...] if more else jnp.zeros_like(sums)
    taken = 0
    for arrays, spans in pieces:
        held = tokens[taken : taken + arrays]
        taken += arrays
        for begin, width, which, offset in spans:
            step = chunk_of(width)

            @pl.loop(0, width // step)
            def _(i, held=held, begin=begin, which=which, offset=offset, step=step):
                at = pl.ds(pl.multiple_of(i * step + begin, 128), step)
                x = jnp.concatenate([h[:, at] for h in held], axis=0)
                w = factors[which][pl.ds(pl.multiple_of(i * step + offset, 128), step), :]
                sums[...] += jnp.dot(x, w, preferred_element_type=jnp.float32)

    if pairs:
        out_ref[...] = by_query(sums[...] * total_of(refs[count + 2 + more : -2]))
    else:
        out_ref[...] = sums[...]


def project_last(groups, factors, start=None, pairs=()):
    pieces = tuple((len(arrays), tuple(spans)) for arrays, spans in groups)
    operands = [a for arrays, _ in groups for a in arrays]
    rows, columns = sum(a.shape[0] for a in groups[0][0]), factors[0].shape[1]
    given = [in_vmem(x) for x in (*operands, *factors)]
    given += ([] if start is None else [start]) + list(pairs)
    return pl.pallas_call(
        functools.partial(project_last_kernel, pieces, int(start is not None), len(pairs)),
        in_specs=[pl.BlockSpec(memory_space=pltpu.VMEM)] * len(given),
        out_specs=pl.BlockSpec(memory_space=pltpu.VMEM),
        out_shape=jax.ShapeDtypeStruct((rows, columns // RANK if pairs else columns), jnp.float32),
        scratch_shapes=[pltpu.VMEM((rows, columns), jnp.float32)],
        compiler_params=params(),
        cost_estimate=LIGHT,
        name="project_last",
    )(*given)


def score_kernel(count, *refs):
    out_ref = refs[-1]
    found = []
    for at in range(0, len(refs) - 1, 1 + count):
        found.append(by_query(refs[at][...] * total_of(refs[at + 1 : at + 1 + count])))
    out_ref[...] = jnp.concatenate(found, axis=0).T


def score(groups):
    rows, columns = sum(one.shape[0] for one, _ in groups), groups[0][0].shape[1]
    return pl.pallas_call(
        functools.partial(score_kernel, len(groups[0][1])),
        out_shape=jax.ShapeDtypeStruct((columns // RANK, rows), jnp.float32),
        compiler_params=params(),
        cost_estimate=LIGHT,
        name="score",
    )(*[x for one, parts in groups for x in (one, *parts)])


def inverse_kernel(*refs):
    gram, out_ref = total_of(refs[:-1]), refs[-1]
    norms = jnp.broadcast_to((gram[0] * gram[1]).sum(axis=0, keepdims=True), (8, gram.shape[2]))
    out_ref[...] = 1.0 / jnp.sqrt(by_query(norms) + 1e-06)


def inverse_norms(parts):
    return pl.pallas_call(
        inverse_kernel,
        out_shape=jax.ShapeDtypeStruct((8, parts[0].shape[2] // RANK), jnp.float32),
        compiler_params=params(),
        cost_estimate=LIGHT,
        name="inverse_norms",
    )(*parts)


def looked_up(table, index):
    return sum(jnp.where(index == i, value, 0) for i, value in enumerate(table))


def last_kernel(count, groups, place, tokens, at_ref, inverse_ref, *refs):
    out_ref, held = refs[-2:]
    chips = len(place)
    for at, distances in enumerate(groups):
        scores = total_of(refs[at * count : (at + 1) * count]).T * inverse_ref[:1]
        first = 0
        for group in distances:
            for c in range(2):
                for distance in group:
                    held[distance % chips, c] = scores[first : first + tokens]
                    first += tokens
    core, side = at_ref[0], at_ref[1]
    here = looked_up(place, core // 2)
    own = core % 2
    share = out_ref.shape[1] // (2 * tokens)
    blocks = []
    for j in range(share):
        there = looked_up(place, side * share + j)
        distance = there - here
        distance = jnp.where(distance < 0, distance + chips, distance)
        blocks += [held[distance, (own + c) % 2] for c in range(2)]
    out_ref[...] = jnp.concatenate(blocks, axis=0).T


def last(results, inverse, groups, place, tokens, share, at):
    queries = inverse.shape[1]
    return pl.pallas_call(
        functools.partial(last_kernel, len(results[0]), groups, place, tokens),
        in_specs=[pl.BlockSpec(memory_space=pltpu.SMEM)]
        + [pl.BlockSpec(memory_space=pltpu.VMEM)] * (1 + sum(len(parts) for parts in results)),
        out_specs=pl.BlockSpec(memory_space=pltpu.VMEM),
        out_shape=jax.ShapeDtypeStruct((queries, share), jnp.float32),
        scratch_shapes=[pltpu.VMEM((len(place), 2, tokens, queries), jnp.float32)],
        compiler_params=params(),
        cost_estimate=LIGHT,
        name="last_scores",
    )(at, inverse, *[x for parts in results for x in parts])


def within(spans, low, high):
    kept = []
    for begin, width, which, offset in spans:
        a, b = max(begin, low), min(begin + width, high)
        if a < b:
            kept.append((a - low, b - a, which, offset + a - begin))
    return kept


def solution(mesh):
    rows = mesh.shape["rows"]
    query = mesh.shape["query"]
    ring = ring_of(mesh)
    chips = len(ring)
    forward = [(a, b) for i in range(chips) for a, b in zip(ring[i], ring[(i + 1) % chips])]
    backward = [(b, a) for a, b in forward]
    mates = [(pair[i], pair[1 - i]) for pair in ring for i in range(2)]
    place = [0] * chips
    for i, pair in enumerate(ring):
        place[pair[0] // 2] = i
    place = tuple(place)

    def swap_rows(x):
        return lax.ppermute(x, "rows", [(0, 1), (1, 0)])

    def across(x):
        return [x, swap_rows(x)] if rows == 2 else [lax.psum(x, "rows")]

    def mate(xs):
        return [lax.ppermute(x, "query", mates) for x in xs]

    def ahead(x):
        return lax.ppermute(x, "query", forward)

    def behind(x):
        return lax.ppermute(x, "query", backward)

    def both(pair):
        return [ahead(pair[0]), behind(pair[1])]

    def tied(*trees):
        return lax.optimization_barrier(trees)

    def local(acts, grads, in_factors, out_factors):
        tokens, width = acts.shape
        depth = grads.shape[1]
        total = width + depth
        step = math.gcd(width, depth)
        while step > 2048 and step % 2 == 0:
            step //= 2
        bounds = [0, depth, depth + width // 2 // step * step, total]
        span = [(0, depth, 1, 0), (depth, width, 0, 0)]
        at = jnp.stack([lax.axis_index("query"), lax.axis_index("rows")]).astype(jnp.int32)
        full_hops = (chips - 1) // 2

        def projected(held):
            swapped = mate(packed(held, bounds, step))
            groups = [
                ([(x, lo) for x in held] + [(part, 0)], within(span, lo, hi))
                for lo, hi, part in zip(bounds, bounds[1:], swapped)]
            return project(groups[1:], factors, step), across(project(groups[:1], factors, step))

        at, acts, grads, in_factors, out_factors = tied(at, acts, grads, in_factors, out_factors)
        own = joined(grads, acts)
        fly = [ahead(own), behind(own)]
        factors = load(in_factors, out_factors)
        gram_parts = across(grams(*factors))
        pairs = [projected([own])]
        distances = [(0,)]
        fly[0], pairs, gram_parts = tied(fly[0], pairs, gram_parts)
        for hop in range(1, full_hops):
            held = list(fly)
            fly[0] = ahead(held[0])
            held = tied(*held)
            fly[1] = behind(held[1])
            pairs.append(projected(held))
            distances.append((-hop, hop))
            fly[0], pairs = tied(fly[0], pairs)
        held = list(fly)
        distances.append((-full_hops, full_hops))
        even = chips % 2 == 0
        if even:
            half = total // 256 * 128
            assert depth < half
            fly = column_ranges(*held, [(0, 0, half), (1, half, total)])
            fly = [ahead(fly[0]), behind(fly[1])]
        pairs.append(projected(held))
        inverse = inverse_norms(gram_parts)
        results = []
        if even:
            inverse, pairs = tied(inverse, pairs)
            early = across(score(pairs))
            low, high, inverse, early = tied(*fly, inverse, early)
            results.append(early)
            swapped = mate([low, high])
            one, two = [low, swapped[0]], [high, swapped[1]]
            other = across(project_last([(one, within(span, 0, depth))], factors))
            mine = project_last(
                [(one, [s for s in within(span, 0, half) if not s[2]]), (two, within(span, half, total))], factors)
            results.append(across(score([(mine, other)])))
            groups = (tuple(distances), ((chips // 2,),))
        else:
            results.append(across(score(pairs)))
            groups = (tuple(distances),)
        return last(results, inverse, groups, place, tokens, query * tokens // rows, at).T

    return jax.shard_map(
        local,
        mesh=mesh,
        in_specs=(P("query", "rows"), P("query", "rows"), P("rows", "query"), P("rows", "query")),
        out_specs=P("rows", "query"),
        check_vma=False,
    )
```

```python
import functools
import math

import jax
import jax.numpy as jnp
from jax import lax
from jax.experimental import pallas as pl
from jax.experimental.pallas import tpu as pltpu
from jax.sharding import PartitionSpec as P

RANK = 32
WIDE = 256
LIGHT = pl.CostEstimate(flops=1, bytes_accessed=1, transcendentals=0)
ROOM = 6 << 20


def params():
    return pltpu.CompilerParams(vmem_limit_bytes=ROOM)


def in_hbm(x):
    return pltpu.with_memory_space_constraint(x, pltpu.HBM)


def in_vmem(x):
    return pltpu.with_memory_space_constraint(x, pltpu.VMEM)


def cycle_of(first, second):
    if min(first, second) == 1:
        size = first * second
        order = list(range(0, size, 2)) + list(range(1, size, 2))[::-1]
        return [(i, 0) if second == 1 else (0, i) for i in order]
    if first % 2:
        return [(a, b) for b, a in cycle_of(second, first)] if second % 2 == 0 else [
            (a, b) for a in range(first) for b in range(second)]
    walk = []
    for a in range(first):
        inner = range(1, second)
        walk += [(a, b) for b in (inner if a % 2 == 0 else reversed(inner))]
    return walk + [(a, 0) for a in reversed(range(first))]


def ring_of(mesh):
    devices = list(mesh.devices[0])
    chips = {}
    for index, device in enumerate(devices):
        coords = getattr(device, "coords", None)
        key = tuple(coords) if coords is not None else (index // 2,)
        chips.setdefault(key, []).append(index)
    keys = list(chips)
    values = [sorted({k[i] for k in keys}) for i in range(len(keys[0]))]
    varying = [i for i in range(len(values)) if len(values[i]) > 1]
    if len(varying) == 2 and len(keys) == len(values[varying[0]]) * len(values[varying[1]]):
        one, two = sorted(varying, key=lambda i: -len(values[i]))
        at = {(values[one].index(k[one]), values[two].index(k[two])): k for k in keys}
        keys = [at[place] for place in cycle_of(len(values[one]), len(values[two]))]
    ring = [chips[k] for k in keys]
    assert all(pair[0] % 2 == 0 and pair[1] == pair[0] + 1 for pair in ring)
    return ring


def chunk_of(*sizes):
    whole = functools.reduce(math.gcd, sizes)
    return next(step for step in range(2048, 0, -128) if whole % step == 0)


def copy_kernel(plan, count, *refs):
    sem = refs[-1]
    copies = [
        pltpu.make_async_copy(
            refs[source].at[:, pl.ds(begin, width)], refs[count + target].at[:, pl.ds(put, width)], sem.at[index])
        for index, (source, begin, target, put, width) in enumerate(plan)]
    for copy in copies:
        copy.start()
    for copy in copies:
        copy.wait()


def columns_of(arrays, outputs, vmem=False):
    kind, space = (pltpu.VMEM, pltpu.VMEM) if vmem else (jax.ShapeDtypeStruct, pl.ANY)
    plan, widths = [], []
    for target, ranges in enumerate(outputs):
        put = 0
        for source, lo, hi in ranges:
            plan.append((source, lo, target, put, hi - lo))
            put += hi - lo
        widths.append(put)
    return pl.pallas_call(
        functools.partial(copy_kernel, tuple(plan), len(arrays)),
        in_specs=[pl.BlockSpec(memory_space=pl.ANY)] * len(arrays),
        out_specs=[pl.BlockSpec(memory_space=space)] * len(outputs),
        out_shape=[kind((arrays[0].shape[0], width), arrays[0].dtype) for width in widths],
        scratch_shapes=[pltpu.SemaphoreType.DMA((len(plan),))],
        compiler_params=params(),
        cost_estimate=LIGHT,
        name="columns",
    )(*arrays)


def load_kernel(step, a_ref, b_ref, a_out, b_out, gram_ref, sums, sem):
    columns = a_ref.shape[1]
    row = lax.broadcasted_iota(jnp.int32, (WIDE, WIDE), 0) // RANK
    col = lax.broadcasted_iota(jnp.int32, (WIDE, WIDE), 1) // RANK
    counts = [a_ref.shape[0] // step, b_ref.shape[0] // step]
    pairs = ((a_ref, a_out), (b_ref, b_out))

    def chunk(index, i):
        source, target = pairs[index]
        at = pl.ds(pl.multiple_of(i * step, step), step)
        return pltpu.make_async_copy(source.at[at], target.at[at], sem.at[index * counts[0] + i])

    for index in range(2):
        for i in range(counts[index]):
            chunk(index, i).start()
    for index in range(2):
        held = pairs[index][1]
        sums[...] = jnp.zeros_like(sums)

        @pl.loop(0, counts[index])
        def _(i, index=index, held=held):
            chunk(index, i).wait()
            for start in range(0, columns, WIDE):
                block = held[pl.ds(pl.multiple_of(i * step, step), step), start : start + WIDE]
                sums[:, start : start + WIDE] += lax.dot_general(
                    block, block, (((0,), (0,)), ((), ())), preferred_element_type=jnp.float32)

        for start in range(0, columns, WIDE):
            kept = jnp.where(row == col, sums[:, start : start + WIDE], 0.0)
            gram_ref[index, :, start : start + WIDE] = kept.reshape(WIDE // RANK, RANK, WIDE).sum(axis=0)


def load(a, b):
    columns = a.shape[1]
    step = chunk_of(math.gcd(a.shape[0], b.shape[0]))
    return pl.pallas_call(
        functools.partial(load_kernel, step),
        in_specs=[pl.BlockSpec(memory_space=pl.ANY)] * 2,
        out_specs=[pl.BlockSpec(memory_space=pltpu.VMEM)] * 3,
        out_shape=[
            pltpu.VMEM(a.shape, a.dtype), pltpu.VMEM(b.shape, b.dtype),
            jax.ShapeDtypeStruct((2, RANK, columns), jnp.float32)],
        scratch_shapes=[
            pltpu.VMEM((WIDE, columns), jnp.float32),
            pltpu.SemaphoreType.DMA(((a.shape[0] + b.shape[0]) // step,))],
        compiler_params=params(),
        cost_estimate=LIGHT,
        name="load_factors",
    )(in_hbm(a), in_hbm(b))


def pack_kernel(count, *refs):
    arrays, out_ref = refs[:count], refs[count]
    packed = jnp.concatenate([x[...] for x in arrays], axis=0)
    for copy in range(2):
        out_ref[copy] = packed


def twice(arrays):
    rows, width = sum(a.shape[0] for a in arrays), arrays[0].shape[1]
    step = chunk_of(width)
    return pl.pallas_call(
        functools.partial(pack_kernel, len(arrays)),
        grid=(width // step,),
        in_specs=[pl.BlockSpec((a.shape[0], step), lambda i: (0, i)) for a in arrays],
        out_specs=pl.BlockSpec((2, rows, step), lambda i: (0, 0, i)),
        out_shape=jax.ShapeDtypeStruct((2, rows, width), arrays[0].dtype),
        compiler_params=params(),
        cost_estimate=LIGHT,
        name="pack",
    )(*arrays)


def beside_kernel(*refs):
    arrays, out_ref, sem = refs[:-2], refs[-2], refs[-1]
    copies, put = [], 0
    for array in arrays:
        for copy in range(2):
            copies.append(pltpu.make_async_copy(
                array, out_ref.at[copy, :, pl.ds(put, array.shape[1])], sem.at[len(copies)]))
        put += array.shape[1]
    for copy in copies:
        copy.start()
    for copy in copies:
        copy.wait()


def beside_twice(arrays):
    shape = (2, arrays[0].shape[0], sum(a.shape[1] for a in arrays))
    return pl.pallas_call(
        beside_kernel,
        in_specs=[pl.BlockSpec(memory_space=pl.ANY)] * len(arrays),
        out_specs=pl.BlockSpec(memory_space=pl.ANY),
        out_shape=jax.ShapeDtypeStruct(shape, arrays[0].dtype),
        scratch_shapes=[pltpu.SemaphoreType.DMA((2 * len(arrays),))],
        compiler_params=params(),
        cost_estimate=LIGHT,
        name="pack",
    )(*arrays)


def project_kernel(step, spans, count, outs, more, *refs):
    held, factors = refs[:count], refs[count : count + 2]
    given, sums = refs[count + 2 : count + 2 + more], refs[-outs:]
    i = pl.program_id(0)

    @pl.when(i == 0)
    def _():
        for index, out in enumerate(sums):
            out[...] = given[index][...] if more else jnp.zeros_like(out)

    for begin, width, which, offset in spans:
        first, steps = begin // step, width // step

        @pl.when((i >= first) & (i < first + steps))
        def _(which=which, offset=offset, first=first):
            x = jnp.concatenate(
                [x for h in held for x in ((h[0], h[1]) if len(h.shape) == 3 else (h[...],))], axis=0)
            at = pl.multiple_of((i - first) * step + offset, step)
            sums[which if outs == 2 else 0][...] += jnp.dot(
                x, factors[which][pl.ds(at, step), :], preferred_element_type=jnp.float32)


def project(arrays, span, factors, outs, start=None):
    width = sum(size for _, size, _, _ in span)
    step = chunk_of(*(size for _, size, _, _ in span))
    shape = (sum(math.prod(a.shape[:-1]) for a in arrays), factors[0].shape[1])
    extra = [] if start is None else [start]
    result = pl.pallas_call(
        functools.partial(project_kernel, step, tuple(span), len(arrays), outs, len(extra)),
        grid=(width // step,),
        in_specs=[
            pl.BlockSpec((*a.shape[:-1], step), lambda i, zeros=(0,) * (a.ndim - 1): (*zeros, i)) for a in arrays]
        + [pl.BlockSpec(memory_space=pltpu.VMEM)] * (2 + len(extra)),
        out_specs=[pl.BlockSpec(shape, lambda i: (0, 0))] * outs,
        out_shape=[jax.ShapeDtypeStruct(shape, jnp.float32)] * outs,
        compiler_params=params(),
        cost_estimate=LIGHT,
        name="project",
    )(*arrays, *[in_vmem(f) for f in factors], *extra)
    return result if outs == 2 else result[0]


def by_query(x):
    columns = x.shape[1]
    queries = columns // RANK
    member = (lax.broadcasted_iota(jnp.int32, (columns, queries), 0) // RANK) == lax.broadcasted_iota(
        jnp.int32, (columns, queries), 1)
    return jnp.dot(
        x, member.astype(jnp.float32), precision=lax.Precision.HIGHEST, preferred_element_type=jnp.float32)


def total_of(refs):
    return sum(ref[...] for ref in refs[1:]) + refs[0][...]


def project_last_kernel(spans, *refs):
    count = len(spans)
    held, mates = refs[:count], refs[count : 2 * count]
    factors, out_ref = refs[2 * count : 2 * count + 2], refs[-1]
    out_ref[...] = jnp.zeros_like(out_ref)
    for mine, other, pieces in zip(held, mates, spans):
        for begin, width, which, offset in pieces:
            step = chunk_of(width)

            @pl.loop(0, width // step)
            def _(i, mine=mine, other=other, begin=begin, which=which, offset=offset, step=step):
                at = pl.ds(pl.multiple_of(i * step + begin, 128), step)
                x = jnp.concatenate([mine[:, at], other[:, at]], axis=0)
                w = factors[which][pl.ds(pl.multiple_of(i * step + offset, 128), step), :]
                out_ref[...] += jnp.dot(x, w, preferred_element_type=jnp.float32)


def project_last(held, mates, spans, factors):
    given = [in_vmem(x) for x in (*held, *mates, *factors)]
    return pl.pallas_call(
        functools.partial(project_last_kernel, tuple(tuple(s) for s in spans)),
        in_specs=[pl.BlockSpec(memory_space=pltpu.VMEM)] * len(given),
        out_specs=pl.BlockSpec(memory_space=pltpu.VMEM),
        out_shape=jax.ShapeDtypeStruct((2 * held[0].shape[0], factors[0].shape[1]), jnp.float32),
        compiler_params=params(),
        cost_estimate=LIGHT,
        name="project_last",
    )(*given)


def score_kernel(counts, earlier, *refs):
    out_ref = refs[-1]
    found, taken = [], earlier
    for count in counts:
        found.append(by_query(refs[taken][...] * total_of(refs[taken + 1 : taken + 1 + count])))
        taken += 1 + count
    out_ref[...] = jnp.concatenate([*[ref[...] for ref in refs[:earlier]], jnp.concatenate(found, axis=0).T], axis=1)


def score(groups, *earlier):
    rows, columns = sum(one.shape[0] for one, _ in groups), groups[0][0].shape[1]
    return pl.pallas_call(
        functools.partial(score_kernel, tuple(len(parts) for _, parts in groups), len(earlier)),
        out_shape=jax.ShapeDtypeStruct((columns // RANK, rows + sum(x.shape[1] for x in earlier)), jnp.float32),
        compiler_params=params(),
        cost_estimate=LIGHT,
        name="score",
    )(*earlier, *[x for one, parts in groups for x in (one, *parts)])


def inverse_kernel(*refs):
    gram, out_ref = total_of(refs[:-1]), refs[-1]
    norms = jnp.broadcast_to((gram[0] * gram[1]).sum(axis=0, keepdims=True), (8, gram.shape[2]))
    out_ref[...] = 1.0 / jnp.sqrt(by_query(norms) + 1e-06)


def inverse_norms(parts):
    return pl.pallas_call(
        inverse_kernel,
        out_shape=jax.ShapeDtypeStruct((8, parts[0].shape[2] // RANK), jnp.float32),
        compiler_params=params(),
        cost_estimate=LIGHT,
        name="inverse_norms",
    )(*parts)


def looked_up(table, index):
    return sum(jnp.where(index == i, value, 0) for i, value in enumerate(table))


def last_kernel(count, groups, place, tokens, at_ref, inverse_ref, *refs):
    out_ref, held = refs[-2:]
    chips = len(place)
    scores = total_of(refs[:count]).T * inverse_ref[:1]
    first = 0
    for group in groups:
        for c in range(2):
            for distance in group:
                core = (at_ref[0] + c) % 2 if distance == chips // 2 else c
                held[distance % chips, core] = scores[first : first + tokens]
                first += tokens
    here = looked_up(place, at_ref[0] // 2)
    side = at_ref[1]
    share = out_ref.shape[1] // (2 * tokens)
    blocks = []
    for j in range(share):
        there = looked_up(place, side * share + j)
        distance = there - here
        distance = jnp.where(distance < 0, distance + chips, distance)
        blocks += [held[distance, c] for c in range(2)]
    out_ref[...] = jnp.concatenate(blocks, axis=0).T


def last(parts, inverse, groups, place, tokens, share, at):
    queries = inverse.shape[1]
    return pl.pallas_call(
        functools.partial(last_kernel, len(parts), groups, place, tokens),
        in_specs=[pl.BlockSpec(memory_space=pltpu.SMEM)] + [pl.BlockSpec(memory_space=pltpu.VMEM)] * (1 + len(parts)),
        out_specs=pl.BlockSpec(memory_space=pltpu.VMEM),
        out_shape=jax.ShapeDtypeStruct((queries, share), jnp.float32),
        scratch_shapes=[pltpu.VMEM((len(place), 2, tokens, queries), jnp.float32)],
        compiler_params=params(),
        cost_estimate=LIGHT,
        name="last_scores",
    )(at, inverse, *parts)


def within(spans, low, high):
    kept = []
    for begin, width, which, offset in spans:
        a, b = max(begin, low), min(begin + width, high)
        if a < b:
            kept.append((a - low, b - a, which, offset + a - begin))
    return kept


def solution(mesh):
    rows = mesh.shape["rows"]
    query = mesh.shape["query"]
    ring = ring_of(mesh)
    chips = len(ring)
    assert chips % 2 == 0 and chips >= 4
    forward = [(a, b) for i in range(chips) for a, b in zip(ring[i], ring[(i + 1) % chips])]
    backward = [(b, a) for a, b in forward]
    mates = [(pair[i], pair[1 - i]) for pair in ring for i in range(2)]
    place = [0] * chips
    for i, pair in enumerate(ring):
        place[pair[0] // 2] = i
    place = tuple(place)

    def across(x):
        if rows == 2:
            return [x, lax.ppermute(x, "rows", [(0, 1), (1, 0)])]
        return [lax.psum(x, "rows")]

    def both_cores(x):
        return lax.all_to_all(x, "query", 0, 0, axis_index_groups=sorted(ring))

    def round_ring(pair):
        return [lax.ppermute(pair[0], "query", forward), lax.ppermute(pair[1], "query", backward)]

    def tied(*trees):
        return lax.optimization_barrier(trees)

    def local(acts, grads, in_factors, out_factors):
        tokens, width = acts.shape
        depth = grads.shape[1]
        half = (width + depth) // 256 * 128
        cut = half - depth
        assert cut > 0
        spans = [[(0, depth, 1, 0), (depth, cut, 0, 0)], [(0, width - cut, 0, cut)]]
        middles = [sum(s[1] for s in span) // 256 * 128 for span in spans]
        at = jnp.stack([lax.axis_index("query"), lax.axis_index("rows")]).astype(jnp.int32)
        last_hop = chips // 2

        def next_of(pair, hop, stream):
            if hop + 1 == last_hop:
                middle = middles[stream]
                pair = columns_of(pair, [[(0, 0, middle)], [(1, middle, pair[1].shape[1])]], True)
            return round_ring(pair)

        at, acts, grads, in_factors, out_factors = tied(at, acts, grads, in_factors, out_factors)
        (own0,) = columns_of([in_hbm(grads), in_hbm(acts)], [[(0, 0, depth), (1, 0, cut)]], True)
        fly0 = round_ring([own0, own0])
        (own1,) = columns_of([in_hbm(acts)], [[(0, cut, width)]], True)
        fly1 = round_ring([own1, own1])
        *factors, gram = load(in_factors, out_factors)
        fly0, own0, own1, gram = tied(fly0, own0, own1, gram)
        groups, pairs, found, gram_parts = [], [], [], []
        for hop in range(1, last_hop):
            extra = hop == 1
            groups.append((-hop, hop) + (0,) * extra)
            held = fly0
            fly0 = next_of(held, hop, 0)
            other, part = project([both_cores(twice(held + [own0] * extra))], spans[0], factors, 2)[::-1]
            if pairs:
                part, pairs, gram = tied(part, pairs, gram)
                found = [score(pairs, *found)]
                gram_parts = gram_parts or across(gram)
            fly1, other, part, found, gram_parts = tied(fly1, other, part, found, gram_parts)
            held = fly1
            fly1 = next_of(held, hop, 1)
            one = project([both_cores(twice(held + [own1] * extra))], spans[1], factors, 1, part)
            other = across(other)
            if hop + 1 < last_hop:
                fly0, one, other = tied(fly0, one, other)
            else:
                fly0, fly1, one, other, gram_parts = tied(fly0, fly1, one, other, gram_parts)
            pairs = [(one, other)]
        groups.append((last_hop,))
        held = [*fly0, *fly1]
        swapped = [lax.ppermute(x, "query", mates) for x in held]
        pieces = [
            within(span, lo, hi)
            for span, middle in zip(spans, middles) for lo, hi in ((0, middle), (middle, sum(s[1] for s in span)))]
        chosen = [[[s for s in piece if s[2] == which] for piece in pieces] for which in range(2)]
        used = [[i for i, piece in enumerate(c) if piece] for c in chosen]
        one, other = [
            project_last([held[i] for i in u], [swapped[i] for i in u], [c[i] for i in u], factors)
            for u, c in zip(used, chosen)]
        found = score(pairs, *found)
        inverse = inverse_norms(gram_parts)
        scores = score([(one, across(other))], found)
        return last(across(scores), inverse, tuple(groups), place, tokens, query * tokens // rows, at).T

    return jax.shard_map(
        local,
        mesh=mesh,
        in_specs=(P("query", "rows"), P("query", "rows"), P("rows", "query"), P("rows", "query")),
        out_specs=P("rows", "query"),
        check_vma=False,
    )
```

```python
import functools
import math

import jax
import jax.numpy as jnp
from jax import lax
from jax.experimental import pallas as pl
from jax.experimental.pallas import tpu as pltpu
from jax.sharding import PartitionSpec as P

RANK = 32
WIDE = 256
LIGHT = pl.CostEstimate(flops=1, bytes_accessed=1, transcendentals=0)
ROOM = 6 << 20


def params():
    return pltpu.CompilerParams(vmem_limit_bytes=ROOM)


def in_hbm(x):
    return pltpu.with_memory_space_constraint(x, pltpu.HBM)


def in_vmem(x):
    return pltpu.with_memory_space_constraint(x, pltpu.VMEM)


def cycle_of(first, second):
    if min(first, second) == 1:
        size = first * second
        order = list(range(0, size, 2)) + list(range(1, size, 2))[::-1]
        return [(i, 0) if second == 1 else (0, i) for i in order]
    if first % 2:
        return [(a, b) for b, a in cycle_of(second, first)] if second % 2 == 0 else [
            (a, b) for a in range(first) for b in range(second)]
    walk = []
    for a in range(first):
        inner = range(1, second)
        walk += [(a, b) for b in (inner if a % 2 == 0 else reversed(inner))]
    return walk + [(a, 0) for a in reversed(range(first))]


def ring_of(mesh):
    devices = list(mesh.devices[0])
    chips = {}
    for index, device in enumerate(devices):
        coords = getattr(device, "coords", None)
        key = tuple(coords) if coords is not None else (index // 2,)
        chips.setdefault(key, []).append(index)
    keys = list(chips)
    values = [sorted({k[i] for k in keys}) for i in range(len(keys[0]))]
    varying = [i for i in range(len(values)) if len(values[i]) > 1]
    if len(varying) == 2 and len(keys) == len(values[varying[0]]) * len(values[varying[1]]):
        one, two = sorted(varying, key=lambda i: -len(values[i]))
        at = {(values[one].index(k[one]), values[two].index(k[two])): k for k in keys}
        keys = [at[place] for place in cycle_of(len(values[one]), len(values[two]))]
    ring = [chips[k] for k in keys]
    assert all(pair[0] % 2 == 0 and pair[1] == pair[0] + 1 for pair in ring)
    return ring


def chunk_of(*sizes):
    whole = functools.reduce(math.gcd, sizes)
    return next(step for step in range(2048, 0, -128) if whole % step == 0)


def copy_kernel(plan, count, *refs):
    sem = refs[-1]
    copies = [
        pltpu.make_async_copy(
            refs[source].at[:, pl.ds(begin, width)], refs[count + target].at[:, pl.ds(put, width)], sem.at[index])
        for index, (source, begin, target, put, width) in enumerate(plan)]
    for copy in copies:
        copy.start()
    for copy in copies:
        copy.wait()


def columns_of(arrays, outputs, vmem=False):
    kind, space = (pltpu.VMEM, pltpu.VMEM) if vmem else (jax.ShapeDtypeStruct, pl.ANY)
    plan, widths = [], []
    for target, ranges in enumerate(outputs):
        put = 0
        for source, lo, hi in ranges:
            plan.append((source, lo, target, put, hi - lo))
            put += hi - lo
        widths.append(put)
    return pl.pallas_call(
        functools.partial(copy_kernel, tuple(plan), len(arrays)),
        in_specs=[pl.BlockSpec(memory_space=pl.ANY)] * len(arrays),
        out_specs=[pl.BlockSpec(memory_space=space)] * len(outputs),
        out_shape=[kind((arrays[0].shape[0], width), arrays[0].dtype) for width in widths],
        scratch_shapes=[pltpu.SemaphoreType.DMA((len(plan),))],
        compiler_params=params(),
        cost_estimate=LIGHT,
        name="columns",
    )(*arrays)


def load_kernel(step, a_ref, b_ref, a_out, b_out, gram_ref, sums, sem):
    columns = a_ref.shape[1]
    row = lax.broadcasted_iota(jnp.int32, (WIDE, WIDE), 0) // RANK
    col = lax.broadcasted_iota(jnp.int32, (WIDE, WIDE), 1) // RANK
    counts = [a_ref.shape[0] // step, b_ref.shape[0] // step]
    pairs = ((a_ref, a_out), (b_ref, b_out))

    def chunk(index, i):
        source, target = pairs[index]
        at = pl.ds(pl.multiple_of(i * step, step), step)
        return pltpu.make_async_copy(source.at[at], target.at[at], sem.at[index * counts[0] + i])

    for index in range(2):
        for i in range(counts[index]):
            chunk(index, i).start()
    for index in range(2):
        held = pairs[index][1]
        sums[...] = jnp.zeros_like(sums)

        @pl.loop(0, counts[index])
        def _(i, index=index, held=held):
            chunk(index, i).wait()
            for start in range(0, columns, WIDE):
                block = held[pl.ds(pl.multiple_of(i * step, step), step), start : start + WIDE]
                sums[:, start : start + WIDE] += lax.dot_general(
                    block, block, (((0,), (0,)), ((), ())), preferred_element_type=jnp.float32)

        for start in range(0, columns, WIDE):
            kept = jnp.where(row == col, sums[:, start : start + WIDE], 0.0)
            gram_ref[index, :, start : start + WIDE] = kept.reshape(WIDE // RANK, RANK, WIDE).sum(axis=0)


def load(a, b):
    columns = a.shape[1]
    step = chunk_of(math.gcd(a.shape[0], b.shape[0]))
    return pl.pallas_call(
        functools.partial(load_kernel, step),
        in_specs=[pl.BlockSpec(memory_space=pl.ANY)] * 2,
        out_specs=[pl.BlockSpec(memory_space=pltpu.VMEM)] * 3,
        out_shape=[
            pltpu.VMEM(a.shape, a.dtype), pltpu.VMEM(b.shape, b.dtype),
            jax.ShapeDtypeStruct((2, RANK, columns), jnp.float32)],
        scratch_shapes=[
            pltpu.VMEM((WIDE, columns), jnp.float32),
            pltpu.SemaphoreType.DMA(((a.shape[0] + b.shape[0]) // step,))],
        compiler_params=params(),
        cost_estimate=LIGHT,
        name="load_factors",
    )(in_hbm(a), in_hbm(b))


def pack_kernel(count, *refs):
    arrays, out_ref = refs[:count], refs[count]
    packed = jnp.concatenate([x[...] for x in arrays], axis=0)
    for copy in range(2):
        out_ref[copy] = packed


def twice(arrays):
    rows, width = sum(a.shape[0] for a in arrays), arrays[0].shape[1]
    step = chunk_of(width)
    return pl.pallas_call(
        functools.partial(pack_kernel, len(arrays)),
        grid=(width // step,),
        in_specs=[pl.BlockSpec((a.shape[0], step), lambda i: (0, i)) for a in arrays],
        out_specs=pl.BlockSpec((2, rows, step), lambda i: (0, 0, i)),
        out_shape=jax.ShapeDtypeStruct((2, rows, width), arrays[0].dtype),
        compiler_params=params(),
        cost_estimate=LIGHT,
        name="pack",
    )(*arrays)


def beside_kernel(*refs):
    arrays, out_ref, sem = refs[:-2], refs[-2], refs[-1]
    copies, put = [], 0
    for array in arrays:
        for copy in range(2):
            copies.append(pltpu.make_async_copy(
                array, out_ref.at[copy, :, pl.ds(put, array.shape[1])], sem.at[len(copies)]))
        put += array.shape[1]
    for copy in copies:
        copy.start()
    for copy in copies:
        copy.wait()


def beside_twice(arrays):
    shape = (2, arrays[0].shape[0], sum(a.shape[1] for a in arrays))
    return pl.pallas_call(
        beside_kernel,
        in_specs=[pl.BlockSpec(memory_space=pl.ANY)] * len(arrays),
        out_specs=pl.BlockSpec(memory_space=pl.ANY),
        out_shape=jax.ShapeDtypeStruct(shape, arrays[0].dtype),
        scratch_shapes=[pltpu.SemaphoreType.DMA((2 * len(arrays),))],
        compiler_params=params(),
        cost_estimate=LIGHT,
        name="pack",
    )(*arrays)


def project_kernel(step, spans, count, outs, more, *refs):
    held, factors = refs[:count], refs[count : count + 2]
    given, sums = refs[count + 2 : count + 2 + more], refs[-outs:]
    i = pl.program_id(0)
    rows = sums[0].shape[0]

    @pl.when(i == 0)
    def _():
        for index, out in enumerate(sums):
            if outs == 1 and more:
                out[...] = given[0][...]
            else:
                out[:rows] = jnp.zeros((rows, out.shape[1]), out.dtype)
        if outs == 2 and more:
            for j in range(2):
                sums[1][rows + j * RANK : rows + (j + 1) * RANK] = given[0][j]

    for begin, width, which, offset in spans:
        first, steps = begin // step, width // step

        @pl.when((i >= first) & (i < first + steps))
        def _(which=which, offset=offset, first=first):
            x = jnp.concatenate(
                [x for h in held for x in ((h[0], h[1]) if len(h.shape) == 3 else (h[...],))], axis=0)
            at = pl.multiple_of((i - first) * step + offset, step)
            sums[which if outs == 2 else 0][:rows] += jnp.dot(
                x, factors[which][pl.ds(at, step), :], preferred_element_type=jnp.float32)


def project(arrays, span, factors, outs, start=None):
    width = sum(size for _, size, _, _ in span)
    step = chunk_of(*(size for _, size, _, _ in span))
    shape = (sum(math.prod(a.shape[:-1]) for a in arrays), factors[0].shape[1])
    extra = [] if start is None else [start]
    shapes = [shape] * outs
    if outs == 2 and extra:
        shapes[1] = (shape[0] + 2 * RANK, shape[1])
    result = pl.pallas_call(
        functools.partial(project_kernel, step, tuple(span), len(arrays), outs, len(extra)),
        grid=(width // step,),
        in_specs=[
            pl.BlockSpec((*a.shape[:-1], step), lambda i, zeros=(0,) * (a.ndim - 1): (*zeros, i)) for a in arrays]
        + [pl.BlockSpec(memory_space=pltpu.VMEM)] * (2 + len(extra)),
        out_specs=[pl.BlockSpec(x, lambda i: (0, 0)) for x in shapes],
        out_shape=[jax.ShapeDtypeStruct(x, jnp.float32) for x in shapes],
        compiler_params=params(),
        cost_estimate=LIGHT,
        name="project",
    )(*arrays, *[in_vmem(f) for f in factors], *extra)
    return result if outs == 2 else result[0]


def by_query(x):
    columns = x.shape[1]
    queries = columns // RANK
    member = (lax.broadcasted_iota(jnp.int32, (columns, queries), 0) // RANK) == lax.broadcasted_iota(
        jnp.int32, (columns, queries), 1)
    return jnp.dot(
        x, member.astype(jnp.float32), precision=lax.Precision.HIGHEST, preferred_element_type=jnp.float32)


def total_of(refs, rows=None):
    return sum(ref[:rows] for ref in refs[1:]) + refs[0][:rows]


def project_last_kernel(plan, counts, *refs):
    arrays, factors = refs[: counts[0]], refs[counts[0] : counts[0] + 2]
    starts, out_ref = refs[counts[0] + 2 : -1], refs[-1]
    if counts[1]:
        first = 0
        for start in starts:
            out_ref[first : first + start.shape[0]] = start[...]
            first += start.shape[0]
    else:
        out_ref[...] = jnp.zeros_like(out_ref)
    for held, width, which, offset in plan:
        step = chunk_of(width)

        @pl.loop(0, width // step)
        def _(i, held=held, which=which, offset=offset, step=step):
            x = []
            for index, begin in held:
                at = pl.ds(pl.multiple_of(i * step + begin, 128), step)
                ref = arrays[index]
                x += [ref[0, :, at], ref[1, :, at]] if len(ref.shape) == 3 else [ref[:, at]]
            w = factors[which][pl.ds(pl.multiple_of(i * step + offset, 128), step), :]
            out_ref[...] += jnp.dot(jnp.concatenate(x, axis=0), w, preferred_element_type=jnp.float32)


def project_last(arrays, plan, factors, starts=()):
    rows = sum(math.prod(arrays[index].shape[:-1]) for index, _ in plan[0][0])
    given = [in_vmem(x) for x in (*arrays, *factors)] + list(starts)
    return pl.pallas_call(
        functools.partial(project_last_kernel, tuple(plan), (len(arrays), len(starts))),
        in_specs=[pl.BlockSpec(memory_space=pltpu.VMEM)] * len(given),
        out_specs=pl.BlockSpec(memory_space=pltpu.VMEM),
        out_shape=jax.ShapeDtypeStruct((rows, factors[0].shape[1]), jnp.float32),
        compiler_params=params(),
        cost_estimate=LIGHT,
        name="project_last",
    )(*given)


def score_kernel(plan, earlier, *refs):
    out_ref = refs[-1]
    one, found, first = refs[earlier][...], [], 0
    taken = earlier + 1
    for count, rows in plan:
        found.append(by_query(one[first : first + rows] * total_of(refs[taken : taken + count], rows)))
        taken += count
        first += rows
    out_ref[...] = jnp.concatenate([*[ref[...] for ref in refs[:earlier]], jnp.concatenate(found, axis=0).T], axis=1)


def score(one, others, earlier=()):
    rows = one.shape[0]
    plan = tuple((len(parts), count) for parts, count in others)
    return pl.pallas_call(
        functools.partial(score_kernel, plan, len(earlier)),
        out_shape=jax.ShapeDtypeStruct(
            (one.shape[1] // RANK, rows + sum(x.shape[1] for x in earlier)), jnp.float32),
        compiler_params=params(),
        cost_estimate=LIGHT,
        name="score",
    )(*earlier, one, *[x for parts, _ in others for x in parts])


def inverse_kernel(*refs):
    out_ref = refs[-1]
    gram = total_of(refs[:-1])[-2 * RANK :]
    norms = jnp.broadcast_to((gram[:RANK] * gram[RANK:]).sum(axis=0, keepdims=True), (8, gram.shape[1]))
    inverse = 1.0 / jnp.sqrt(by_query(norms) + 1e-06)
    out_ref[...] = jnp.broadcast_to(inverse.T[:, :1], out_ref.shape)


def inverse_norms(parts):
    return pl.pallas_call(
        inverse_kernel,
        out_shape=jax.ShapeDtypeStruct((parts[0].shape[1] // RANK, 128), jnp.float32),
        compiler_params=params(),
        cost_estimate=LIGHT,
        name="inverse_norms",
    )(*parts)


def looked_up(table, index):
    return sum(jnp.where(index == i, value, 0) for i, value in enumerate(table))


def last_kernel(count, groups, place, tokens, inverse_ref, *refs):
    out_ref = refs[-1]
    chips = len(place)
    scores = jnp.concatenate([total_of(refs[i : i + count]) for i in range(0, len(refs) - 1, count)], axis=1)
    width = scores.shape[1]
    starts = [[0] * chips for _ in range(2)]
    first = 0
    for group in groups:
        for c in range(2):
            for distance in group:
                starts[c][distance % chips] = first
                first += tokens
    query_at, side = lax.axis_index("query"), lax.axis_index("rows")
    core = query_at % 2
    here = looked_up(place, query_at // 2)
    share = out_ref.shape[1] // (2 * tokens)
    lane = lax.broadcasted_iota(jnp.int32, scores.shape, 1) // tokens
    result = jnp.zeros_like(scores)
    for j in range(share):
        distance = looked_up(place, side * share + j) - here
        distance = jnp.where(distance < 0, distance + chips, distance)
        firsts = [looked_up(starts[c], distance) for c in range(2)]
        turned = (distance == chips // 2) & (core == 1)
        firsts = [jnp.where(turned, firsts[1 - c], firsts[c]) for c in range(2)]
        for c in range(2):
            shift = (2 * j + c) * tokens - firsts[c]
            shift = jnp.where(shift < 0, shift + width, shift)
            result = jnp.where(lane == 2 * j + c, pltpu.roll(scores, shift, 1), result)
    out_ref[...] = result[:, : out_ref.shape[1]] * inverse_ref[:, :1]


def last(results, inverse, groups, place, tokens, share):
    return pl.pallas_call(
        functools.partial(last_kernel, len(results[0]), groups, place, tokens),
        in_specs=[pl.BlockSpec(memory_space=pltpu.VMEM)] * (1 + sum(len(parts) for parts in results)),
        out_specs=pl.BlockSpec(memory_space=pltpu.VMEM),
        out_shape=jax.ShapeDtypeStruct((inverse.shape[0], share), jnp.float32),
        compiler_params=params(),
        cost_estimate=LIGHT,
        name="last_scores",
    )(inverse, *[x for parts in results for x in parts])


def solution(mesh):
    rows = mesh.shape["rows"]
    query = mesh.shape["query"]
    ring = ring_of(mesh)
    chips = len(ring)
    assert chips % 2 == 0 and chips >= 4
    forward = [(a, b) for i in range(chips) for a, b in zip(ring[i], ring[(i + 1) % chips])]
    backward = [(b, a) for a, b in forward]
    mates = [(pair[i], pair[1 - i]) for pair in ring for i in range(2)]
    place = [0] * chips
    for i, pair in enumerate(ring):
        place[pair[0] // 2] = i
    place = tuple(place)

    def across(x):
        if rows == 2:
            return [x, lax.ppermute(x, "rows", [(0, 1), (1, 0)])]
        return [lax.psum(x, "rows")]

    def both_cores(x):
        return lax.all_to_all(x, "query", 0, 0, axis_index_groups=sorted(ring))

    def mate(xs):
        return [lax.ppermute(x, "query", mates) for x in xs]

    def round_ring(pair):
        return [lax.ppermute(pair[0], "query", forward), lax.ppermute(pair[1], "query", backward)]

    def tied(*trees):
        return lax.optimization_barrier(trees)

    def local(acts, grads, in_factors, out_factors):
        tokens, width = acts.shape
        depth = grads.shape[1]
        half = (width + depth) // 256 * 128
        cut = half - depth
        assert cut > 0
        spans = [[(0, depth, 1, 0), (depth, cut, 0, 0)], [(0, width - cut, 0, cut)]]
        last_hop = chips // 2

        (own0,) = columns_of([in_hbm(grads), in_hbm(acts)], [[(0, 0, depth), (1, 0, cut)]], True)
        fly0 = round_ring([own0, own0])
        (own1,) = columns_of([in_hbm(acts)], [[(0, cut, width)]], True)
        fly1 = round_ring([own1, own1])
        *factors, gram = load(in_factors, out_factors)
        fly0, own0, own1, gram = tied(fly0, own0, own1, gram)
        groups, pair, found = [], [], []
        for hop in range(1, last_hop):
            extra = hop == 1
            final = hop + 1 == last_hop
            groups.append((-hop, hop) + (0,) * extra)
            held0 = fly0
            if final:
                middle, low = depth // 256 * 128, cut // 256 * 128
                fly0 = columns_of(held0, [
                    [(0, 0, middle), (0, depth, depth + low)], [(1, middle, depth), (1, depth + low, half)]], True)
            fly0 = round_ring(fly0)
            other, part = project(
                [both_cores(twice(held0 + [own0] * extra))], spans[0], factors, 2,
                gram if hop == min(2, last_hop - 1) else None)[::-1]
            if pair:
                part, pair = tied(part, pair)
                found = [score(pair[0], [(pair[1], pair[0].shape[0])], found)]
            fly1, other, part, found = tied(fly1, other, part, found)
            held1 = fly1
            if final:
                high = (width - cut) // 256 * 128
                fly1 = columns_of(held1, [[(0, 0, high)], [(1, high, width - cut)]], True)
            fly1 = round_ring(fly1)
            swapped = both_cores(twice(held1 + [own1] * extra))
            if final:
                other = across(other)
                fly0, swapped, other, part = tied(fly0, swapped, other, part)
            else:
                one = project([swapped], spans[1], factors, 1, part)
                other = across(other)
                fly0, one, other = tied(fly0, one, other)
                pair = (one, other)
            if hop == min(2, last_hop - 1):
                gram_parts = other
        groups.append((last_hop,))
        arrays = [swapped]
        held = columns_of(fly0, [
            [(0, 0, middle), (1, 0, depth - middle)],
            [(0, middle, middle + low)], [(1, depth - middle, half - middle - low)]], True)
        swapped = mate(held)
        last_other = project_last([held[0], swapped[0]], [(((0, 0), (1, 0)), depth, 1, 0)], factors)
        last_part = project_last([*held[1:], *swapped[1:]], [
            (((0, 0), (2, 0)), low, 0, 0), (((1, 0), (3, 0)), cut - low, 0, low)], factors)
        inverse = inverse_norms(gram_parts)
        results = [across(x) for x in found]
        fly1, arrays, part, last_part, last_other, inverse, results = tied(
            fly1, arrays, part, last_part, last_other, inverse, results)
        swapped = mate(fly1)
        last_other = across(last_other)
        one = project_last([*arrays, *fly1, *swapped], [
            (((0, 0), (1, 0), (3, 0)), high, 0, cut),
            (((0, high), (2, 0), (4, 0)), width - cut - high, 0, cut + high)], factors, [part, last_part])
        results.append(across(score(one, [(other, part.shape[0]), (last_other, 2 * tokens)])))
        return last(results, inverse, tuple(groups), place, tokens, query * tokens // rows).T

    return jax.shard_map(
        local,
        mesh=mesh,
        in_specs=(P("query", "rows"), P("query", "rows"), P("rows", "query"), P("rows", "query")),
        out_specs=P("rows", "query"),
        check_vma=False,
    )
```

```python
import functools
import math

import jax
import jax.numpy as jnp
from jax import lax
from jax.experimental import pallas as pl
from jax.experimental.pallas import tpu as pltpu
from jax.sharding import PartitionSpec as P

RANK = 32
WIDE = 256
LIGHT = pl.CostEstimate(flops=1, bytes_accessed=1, transcendentals=0)
ROOM = 6 << 20


def params():
    return pltpu.CompilerParams(vmem_limit_bytes=ROOM)


def in_hbm(x):
    return pltpu.with_memory_space_constraint(x, pltpu.HBM)


def in_vmem(x):
    return pltpu.with_memory_space_constraint(x, pltpu.VMEM)


def cycle_of(first, second):
    if min(first, second) == 1:
        size = first * second
        order = list(range(0, size, 2)) + list(range(1, size, 2))[::-1]
        return [(i, 0) if second == 1 else (0, i) for i in order]
    if first % 2:
        return [(a, b) for b, a in cycle_of(second, first)] if second % 2 == 0 else [
            (a, b) for a in range(first) for b in range(second)]
    walk = []
    for a in range(first):
        inner = range(1, second)
        walk += [(a, b) for b in (inner if a % 2 == 0 else reversed(inner))]
    return walk + [(a, 0) for a in reversed(range(first))]


def ring_of(mesh):
    devices = list(mesh.devices[0])
    chips = {}
    for index, device in enumerate(devices):
        coords = getattr(device, "coords", None)
        key = tuple(coords) if coords is not None else (index // 2,)
        chips.setdefault(key, []).append(index)
    keys = list(chips)
    values = [sorted({k[i] for k in keys}) for i in range(len(keys[0]))]
    varying = [i for i in range(len(values)) if len(values[i]) > 1]
    if len(varying) == 2 and len(keys) == len(values[varying[0]]) * len(values[varying[1]]):
        one, two = sorted(varying, key=lambda i: -len(values[i]))
        at = {(values[one].index(k[one]), values[two].index(k[two])): k for k in keys}
        keys = [at[place] for place in cycle_of(len(values[one]), len(values[two]))]
    ring = [chips[k] for k in keys]
    assert all(pair[0] % 2 == 0 and pair[1] == pair[0] + 1 for pair in ring)
    return ring


def chunk_of(*sizes):
    whole = functools.reduce(math.gcd, sizes)
    return next(step for step in range(2048, 0, -128) if whole % step == 0)


def copy_kernel(plan, count, *refs):
    sem = refs[-1]
    copies = [
        pltpu.make_async_copy(
            refs[source].at[:, pl.ds(begin, width)], refs[count + target].at[:, pl.ds(put, width)], sem.at[index])
        for index, (source, begin, target, put, width) in enumerate(plan)]
    for copy in copies:
        copy.start()
    for copy in copies:
        copy.wait()


def columns_of(arrays, outputs, vmem=False):
    kind, space = (pltpu.VMEM, pltpu.VMEM) if vmem else (jax.ShapeDtypeStruct, pl.ANY)
    plan, widths = [], []
    for target, ranges in enumerate(outputs):
        put = 0
        for source, lo, hi in ranges:
            plan.append((source, lo, target, put, hi - lo))
            put += hi - lo
        widths.append(put)
    return pl.pallas_call(
        functools.partial(copy_kernel, tuple(plan), len(arrays)),
        in_specs=[pl.BlockSpec(memory_space=pl.ANY)] * len(arrays),
        out_specs=[pl.BlockSpec(memory_space=space)] * len(outputs),
        out_shape=[kind((arrays[0].shape[0], width), arrays[0].dtype) for width in widths],
        scratch_shapes=[pltpu.SemaphoreType.DMA((len(plan),))],
        compiler_params=params(),
        cost_estimate=LIGHT,
        name="columns",
    )(*arrays)


def load_kernel(step, a_ref, b_ref, a_out, b_out, gram_ref, sums, sem):
    columns = a_ref.shape[1]
    row = lax.broadcasted_iota(jnp.int32, (WIDE, WIDE), 0) // RANK
    col = lax.broadcasted_iota(jnp.int32, (WIDE, WIDE), 1) // RANK
    counts = [a_ref.shape[0] // step, b_ref.shape[0] // step]
    pairs = ((a_ref, a_out), (b_ref, b_out))

    def chunk(index, i):
        source, target = pairs[index]
        at = pl.ds(pl.multiple_of(i * step, step), step)
        return pltpu.make_async_copy(source.at[at], target.at[at], sem.at[index * counts[0] + i])

    for index in range(2):
        for i in range(counts[index]):
            chunk(index, i).start()
    for index in range(2):
        held = pairs[index][1]
        sums[...] = jnp.zeros_like(sums)

        @pl.loop(0, counts[index])
        def _(i, index=index, held=held):
            chunk(index, i).wait()
            for start in range(0, columns, WIDE):
                block = held[pl.ds(pl.multiple_of(i * step, step), step), start : start + WIDE]
                sums[:, start : start + WIDE] += lax.dot_general(
                    block, block, (((0,), (0,)), ((), ())), preferred_element_type=jnp.float32)

        for start in range(0, columns, WIDE):
            kept = jnp.where(row == col, sums[:, start : start + WIDE], 0.0)
            gram_ref[index, :, start : start + WIDE] = kept.reshape(WIDE // RANK, RANK, WIDE).sum(axis=0)


def load(a, b):
    columns = a.shape[1]
    step = chunk_of(math.gcd(a.shape[0], b.shape[0]))
    return pl.pallas_call(
        functools.partial(load_kernel, step),
        in_specs=[pl.BlockSpec(memory_space=pl.ANY)] * 2,
        out_specs=[pl.BlockSpec(memory_space=pltpu.VMEM)] * 3,
        out_shape=[
            pltpu.VMEM(a.shape, a.dtype), pltpu.VMEM(b.shape, b.dtype),
            jax.ShapeDtypeStruct((2, RANK, columns), jnp.float32)],
        scratch_shapes=[
            pltpu.VMEM((WIDE, columns), jnp.float32),
            pltpu.SemaphoreType.DMA(((a.shape[0] + b.shape[0]) // step,))],
        compiler_params=params(),
        cost_estimate=LIGHT,
        name="load_factors",
    )(in_hbm(a), in_hbm(b))


def pack_kernel(count, *refs):
    arrays, out_ref = refs[:count], refs[count]
    packed = jnp.concatenate([x[...] for x in arrays], axis=0)
    for copy in range(2):
        out_ref[copy] = packed


def twice(arrays):
    rows, width = sum(a.shape[0] for a in arrays), arrays[0].shape[1]
    step = chunk_of(width)
    return pl.pallas_call(
        functools.partial(pack_kernel, len(arrays)),
        grid=(width // step,),
        in_specs=[pl.BlockSpec((a.shape[0], step), lambda i: (0, i)) for a in arrays],
        out_specs=pl.BlockSpec((2, rows, step), lambda i: (0, 0, i)),
        out_shape=jax.ShapeDtypeStruct((2, rows, width), arrays[0].dtype),
        compiler_params=params(),
        cost_estimate=LIGHT,
        name="pack",
    )(*arrays)


def beside_kernel(*refs):
    arrays, out_ref, sem = refs[:-2], refs[-2], refs[-1]
    copies, put = [], 0
    for array in arrays:
        for copy in range(2):
            copies.append(pltpu.make_async_copy(
                array, out_ref.at[copy, :, pl.ds(put, array.shape[1])], sem.at[len(copies)]))
        put += array.shape[1]
    for copy in copies:
        copy.start()
    for copy in copies:
        copy.wait()


def beside_twice(arrays):
    shape = (2, arrays[0].shape[0], sum(a.shape[1] for a in arrays))
    return pl.pallas_call(
        beside_kernel,
        in_specs=[pl.BlockSpec(memory_space=pl.ANY)] * len(arrays),
        out_specs=pl.BlockSpec(memory_space=pl.ANY),
        out_shape=jax.ShapeDtypeStruct(shape, arrays[0].dtype),
        scratch_shapes=[pltpu.SemaphoreType.DMA((2 * len(arrays),))],
        compiler_params=params(),
        cost_estimate=LIGHT,
        name="pack",
    )(*arrays)


def project_kernel(step, spans, count, outs, more, *refs):
    held, factors = refs[:count], refs[count : count + 2]
    given, sums = refs[count + 2 : count + 2 + more], refs[-outs:]
    i = pl.program_id(0)
    rows = sums[0].shape[0]

    @pl.when(i == 0)
    def _():
        for index, out in enumerate(sums):
            if outs == 1 and more:
                out[...] = given[0][...]
            else:
                out[:rows] = jnp.zeros((rows, out.shape[1]), out.dtype)
        if outs == 2 and more:
            for j in range(2):
                sums[1][rows + j * RANK : rows + (j + 1) * RANK] = given[0][j]

    for begin, width, which, offset in spans:
        first, steps = begin // step, width // step

        @pl.when((i >= first) & (i < first + steps))
        def _(which=which, offset=offset, first=first):
            x = jnp.concatenate(
                [x for h in held for x in ((h[0], h[1]) if len(h.shape) == 3 else (h[...],))], axis=0)
            at = pl.multiple_of((i - first) * step + offset, step)
            sums[which if outs == 2 else 0][:rows] += jnp.dot(
                x, factors[which][pl.ds(at, step), :], preferred_element_type=jnp.float32)


def project(arrays, span, factors, outs, start=None):
    width = sum(size for _, size, _, _ in span)
    step = chunk_of(*(size for _, size, _, _ in span))
    shape = (sum(math.prod(a.shape[:-1]) for a in arrays), factors[0].shape[1])
    extra = [] if start is None else [start]
    shapes = [shape] * outs
    if outs == 2 and extra:
        shapes[1] = (shape[0] + 2 * RANK, shape[1])
    result = pl.pallas_call(
        functools.partial(project_kernel, step, tuple(span), len(arrays), outs, len(extra)),
        grid=(width // step,),
        in_specs=[
            pl.BlockSpec((*a.shape[:-1], step), lambda i, zeros=(0,) * (a.ndim - 1): (*zeros, i)) for a in arrays]
        + [pl.BlockSpec(memory_space=pltpu.VMEM)] * (2 + len(extra)),
        out_specs=[pl.BlockSpec(x, lambda i: (0, 0)) for x in shapes],
        out_shape=[jax.ShapeDtypeStruct(x, jnp.float32) for x in shapes],
        compiler_params=params(),
        cost_estimate=LIGHT,
        name="project",
    )(*arrays, *[in_vmem(f) for f in factors], *extra)
    return result if outs == 2 else result[0]


def by_query(x):
    columns = x.shape[1]
    queries = columns // RANK
    member = (lax.broadcasted_iota(jnp.int32, (columns, queries), 0) // RANK) == lax.broadcasted_iota(
        jnp.int32, (columns, queries), 1)
    return jnp.dot(
        x, member.astype(jnp.float32), precision=lax.Precision.HIGHEST, preferred_element_type=jnp.float32)


def total_of(refs, rows=None):
    return sum(ref[:rows] for ref in refs[1:]) + refs[0][:rows]


def project_last_kernel(plan, counts, *refs):
    arrays, factors = refs[: counts[0]], refs[counts[0] : counts[0] + 2]
    starts, out_ref = refs[counts[0] + 2 : -1], refs[-1]
    if counts[1]:
        first = 0
        for start in starts:
            out_ref[first : first + start.shape[0]] = start[...]
            first += start.shape[0]
    else:
        out_ref[...] = jnp.zeros_like(out_ref)
    for held, width, which, offset in plan:
        step = chunk_of(width)

        @pl.loop(0, width // step)
        def _(i, held=held, which=which, offset=offset, step=step):
            x = []
            for index, begin in held:
                at = pl.ds(pl.multiple_of(i * step + begin, 128), step)
                ref = arrays[index]
                x += [ref[0, :, at], ref[1, :, at]] if len(ref.shape) == 3 else [ref[:, at]]
            w = factors[which][pl.ds(pl.multiple_of(i * step + offset, 128), step), :]
            out_ref[...] += jnp.dot(jnp.concatenate(x, axis=0), w, preferred_element_type=jnp.float32)


def project_last(arrays, plan, factors, starts=()):
    rows = sum(math.prod(arrays[index].shape[:-1]) for index, _ in plan[0][0])
    given = [in_vmem(x) for x in (*arrays, *factors)] + list(starts)
    return pl.pallas_call(
        functools.partial(project_last_kernel, tuple(plan), (len(arrays), len(starts))),
        in_specs=[pl.BlockSpec(memory_space=pltpu.VMEM)] * len(given),
        out_specs=pl.BlockSpec(memory_space=pltpu.VMEM),
        out_shape=jax.ShapeDtypeStruct((rows, factors[0].shape[1]), jnp.float32),
        compiler_params=params(),
        cost_estimate=LIGHT,
        name="project_last",
    )(*given)


def score_kernel(plan, earlier, *refs):
    out_ref = refs[-1]
    one, found, first = refs[earlier][...], [], 0
    taken = earlier + 1
    for count, rows in plan:
        found.append(by_query(one[first : first + rows] * total_of(refs[taken : taken + count], rows)))
        taken += count
        first += rows
    out_ref[...] = jnp.concatenate([*[ref[...] for ref in refs[:earlier]], jnp.concatenate(found, axis=0).T], axis=1)


def score(one, others, earlier=()):
    rows = one.shape[0]
    plan = tuple((len(parts), count) for parts, count in others)
    return pl.pallas_call(
        functools.partial(score_kernel, plan, len(earlier)),
        out_shape=jax.ShapeDtypeStruct(
            (one.shape[1] // RANK, rows + sum(x.shape[1] for x in earlier)), jnp.float32),
        compiler_params=params(),
        cost_estimate=LIGHT,
        name="score",
    )(*earlier, one, *[x for parts, _ in others for x in parts])


def inverse_kernel(*refs):
    out_ref = refs[-1]
    gram = total_of(refs[:-1])
    first, second = (gram[0], gram[1]) if gram.ndim == 3 else (gram[-2 * RANK : -RANK], gram[-RANK:])
    norms = jnp.broadcast_to((first * second).sum(axis=0, keepdims=True), (8, gram.shape[-1]))
    inverse = 1.0 / jnp.sqrt(by_query(norms) + 1e-06)
    out_ref[...] = jnp.broadcast_to(inverse.T[:, :1], out_ref.shape)


def inverse_norms(parts):
    return pl.pallas_call(
        inverse_kernel,
        out_shape=jax.ShapeDtypeStruct((parts[0].shape[-1] // RANK, 128), jnp.float32),
        compiler_params=params(),
        cost_estimate=LIGHT,
        name="inverse_norms",
    )(*parts)


def looked_up(table, index):
    return sum(jnp.where(index == i, value, 0) for i, value in enumerate(table))


def last_kernel(groups, place, tokens, inverse_ref, *refs):
    out_ref = refs[-1]
    chips = len(place)
    scores = total_of(refs[:-1])
    width = scores.shape[1]
    starts = [[0] * chips for _ in range(2)]
    first = 0
    for group in groups:
        for c in range(2):
            for distance in group:
                starts[c][distance % chips] = first
                first += tokens
    query_at, side = lax.axis_index("query"), lax.axis_index("rows")
    core = query_at % 2
    here = looked_up(place, query_at // 2)
    share = out_ref.shape[1] // (2 * tokens)
    lane = lax.broadcasted_iota(jnp.int32, scores.shape, 1) // tokens
    result = jnp.zeros_like(scores)
    for j in range(share):
        distance = looked_up(place, side * share + j) - here
        distance = jnp.where(distance < 0, distance + chips, distance)
        firsts = [looked_up(starts[c], distance) for c in range(2)]
        turned = (distance == chips // 2) & (core == 1)
        firsts = [jnp.where(turned, firsts[1 - c], firsts[c]) for c in range(2)]
        for c in range(2):
            shift = (2 * j + c) * tokens - firsts[c]
            shift = jnp.where(shift < 0, shift + width, shift)
            result = jnp.where(lane == 2 * j + c, pltpu.roll(scores, shift, 1), result)
    out_ref[...] = result[:, : out_ref.shape[1]] * inverse_ref[:, :1]


def last(parts, inverse, groups, place, tokens, share):
    return pl.pallas_call(
        functools.partial(last_kernel, groups, place, tokens),
        in_specs=[pl.BlockSpec(memory_space=pltpu.VMEM)] * (1 + len(parts)),
        out_specs=pl.BlockSpec(memory_space=pltpu.VMEM),
        out_shape=jax.ShapeDtypeStruct((inverse.shape[0], share), jnp.float32),
        compiler_params=params(),
        cost_estimate=LIGHT,
        name="last_scores",
    )(inverse, *parts)


def solution(mesh):
    rows = mesh.shape["rows"]
    query = mesh.shape["query"]
    ring = ring_of(mesh)
    chips = len(ring)
    assert chips % 2 == 0 and chips >= 4
    forward = [(a, b) for i in range(chips) for a, b in zip(ring[i], ring[(i + 1) % chips])]
    backward = [(b, a) for a, b in forward]
    mates = [(pair[i], pair[1 - i]) for pair in ring for i in range(2)]
    place = [0] * chips
    for i, pair in enumerate(ring):
        place[pair[0] // 2] = i
    place = tuple(place)

    def across(x):
        if rows == 2:
            return [x, lax.ppermute(x, "rows", [(0, 1), (1, 0)])]
        return [lax.psum(x, "rows")]

    def both_cores(x):
        return lax.all_to_all(x, "query", 0, 0, axis_index_groups=sorted(ring))

    def mate(xs):
        return [lax.ppermute(x, "query", mates) for x in xs]

    def round_ring(pair):
        return [lax.ppermute(pair[0], "query", forward), lax.ppermute(pair[1], "query", backward)]

    def tied(*trees):
        return lax.optimization_barrier(trees)

    def local(acts, grads, in_factors, out_factors):
        tokens, width = acts.shape
        depth = grads.shape[1]
        half = (width + depth) // 256 * 128
        cut = half - depth
        assert cut > 0
        spans = [[(0, depth, 1, 0), (depth, cut, 0, 0)], [(0, width - cut, 0, cut)]]
        last_hop = chips // 2

        (own0,) = columns_of([in_hbm(grads), in_hbm(acts)], [[(0, 0, depth), (1, 0, cut)]], True)
        fly0 = round_ring([own0, own0])
        (own1,) = columns_of([in_hbm(acts)], [[(0, cut, width)]], True)
        fly1 = round_ring([own1, own1])
        *factors, gram = load(in_factors, out_factors)
        fly0, own0, own1, gram = tied(fly0, own0, own1, gram)
        groups, pair, found, gram_parts = [], [], [], []
        for hop in range(1, last_hop):
            extra = hop == 1
            final = hop + 1 == last_hop
            groups.append((-hop, hop) + (0,) * extra)
            held0 = fly0
            if final:
                middle, low = depth // 256 * 128, cut // 256 * 128
                fly0 = columns_of(held0, [
                    [(0, 0, middle), (0, depth, depth + low)], [(1, middle, depth), (1, depth + low, half)]], True)
            fly0 = round_ring(fly0)
            other, part = project(
                [both_cores(twice(held0 + [own0] * extra))], spans[0], factors, 2,
                gram if hop == 2 and not final else None)[::-1]
            if pair:
                part, pair, gram_parts = tied(part, pair, gram_parts)
                found = [score(pair[0], [(pair[1], pair[0].shape[0])], found)]
            if final:
                inverse = inverse_norms(gram_parts or across(gram))
                found.append(inverse)
            fly1, other, part, found = tied(fly1, other, part, found)
            held1 = fly1
            if final:
                high = (width - cut) // 256 * 128 + (width - cut) // 24 // 128 * 128
                fly1 = columns_of(held1, [[(0, 0, high)], [(1, high, width - cut)]], True)
            fly1 = round_ring(fly1)
            swapped = both_cores(twice(held1 + [own1] * extra))
            if final:
                other = across(other)
                fly0, swapped, other, part = tied(fly0, swapped, other, part)
            else:
                one = project([swapped], spans[1], factors, 1, part)
                other = across(other)
                fly0, one, other = tied(fly0, one, other)
                pair = (one, other)
            if hop == 2 and not final:
                gram_parts = other
        groups.append((last_hop,))
        arrays = [swapped]
        held = columns_of(fly0, [
            [(0, 0, middle), (1, 0, depth - middle)],
            [(0, middle, middle + low)], [(1, depth - middle, half - middle - low)]], True)
        swapped = mate(held)
        last_other = project_last([held[0], swapped[0]], [(((0, 0), (1, 0)), depth, 1, 0)], factors)
        *found, inverse = found
        fly1, arrays, part, held, swapped, last_other, inverse, found = tied(
            fly1, arrays, part, held, swapped, last_other, inverse, found)
        last_part = project_last([*held[1:], *swapped[1:]], [
            (((0, 0), (2, 0)), low, 0, 0), (((1, 0), (3, 0)), cut - low, 0, low)], factors)
        swapped = mate(fly1)
        last_other = across(last_other)
        fly1, swapped, last_part = tied(fly1, swapped, last_part)
        one = project_last([*arrays, *fly1, *swapped], [
            (((0, 0), (1, 0), (3, 0)), high, 0, cut),
            (((0, high), (2, 0), (4, 0)), width - cut - high, 0, cut + high)], factors, [part, last_part])
        results = across(score(one, [(other, part.shape[0]), (last_other, 2 * tokens)], found))
        return last(results, inverse, tuple(groups), place, tokens, query * tokens // rows).T

    return jax.shard_map(
        local,
        mesh=mesh,
        in_specs=(P("query", "rows"), P("query", "rows"), P("rows", "query"), P("rows", "query")),
        out_specs=P("rows", "query"),
        check_vma=False,
    )
```

```python
import functools
import math

import jax
import jax.numpy as jnp
from jax import lax
from jax.experimental import pallas as pl
from jax.experimental.pallas import tpu as pltpu
from jax.sharding import PartitionSpec as P

RANK = 32
WIDE = 256
LIGHT = pl.CostEstimate(flops=1, bytes_accessed=1, transcendentals=0)
ROOM = 6 << 20


def params():
    return pltpu.CompilerParams(vmem_limit_bytes=ROOM)


def in_hbm(x):
    return pltpu.with_memory_space_constraint(x, pltpu.HBM)


def in_vmem(x):
    return pltpu.with_memory_space_constraint(x, pltpu.VMEM)


def cycle_of(first, second):
    if min(first, second) == 1:
        size = first * second
        order = list(range(0, size, 2)) + list(range(1, size, 2))[::-1]
        return [(i, 0) if second == 1 else (0, i) for i in order]
    if first % 2:
        return [(a, b) for b, a in cycle_of(second, first)] if second % 2 == 0 else [
            (a, b) for a in range(first) for b in range(second)]
    walk = []
    for a in range(first):
        inner = range(1, second)
        walk += [(a, b) for b in (inner if a % 2 == 0 else reversed(inner))]
    return walk + [(a, 0) for a in reversed(range(first))]


def ring_of(mesh):
    devices = list(mesh.devices[0])
    chips = {}
    for index, device in enumerate(devices):
        coords = getattr(device, "coords", None)
        key = tuple(coords) if coords is not None else (index // 2,)
        chips.setdefault(key, []).append(index)
    keys = list(chips)
    values = [sorted({k[i] for k in keys}) for i in range(len(keys[0]))]
    varying = [i for i in range(len(values)) if len(values[i]) > 1]
    if len(varying) == 2 and len(keys) == len(values[varying[0]]) * len(values[varying[1]]):
        one, two = sorted(varying, key=lambda i: -len(values[i]))
        at = {(values[one].index(k[one]), values[two].index(k[two])): k for k in keys}
        keys = [at[place] for place in cycle_of(len(values[one]), len(values[two]))]
    ring = [chips[k] for k in keys]
    assert all(pair[0] % 2 == 0 and pair[1] == pair[0] + 1 for pair in ring)
    return ring


def chunk_of(*sizes, most=2048):
    whole = functools.reduce(math.gcd, sizes)
    return next(step for step in range(most, 0, -128) if whole % step == 0)


def copy_kernel(plan, count, *refs):
    sem = refs[-1]
    copies = [
        pltpu.make_async_copy(
            refs[source].at[:, pl.ds(begin, width)], refs[count + target].at[:, pl.ds(put, width)], sem.at[index])
        for index, (source, begin, target, put, width) in enumerate(plan)]
    for copy in copies:
        copy.start()
    for copy in copies:
        copy.wait()


def columns_of(arrays, outputs, vmem=False):
    kind, space = (pltpu.VMEM, pltpu.VMEM) if vmem else (jax.ShapeDtypeStruct, pl.ANY)
    plan, widths = [], []
    for target, ranges in enumerate(outputs):
        put = 0
        for source, lo, hi in ranges:
            plan.append((source, lo, target, put, hi - lo))
            put += hi - lo
        widths.append(put)
    return pl.pallas_call(
        functools.partial(copy_kernel, tuple(plan), len(arrays)),
        in_specs=[pl.BlockSpec(memory_space=pl.ANY)] * len(arrays),
        out_specs=[pl.BlockSpec(memory_space=space)] * len(outputs),
        out_shape=[kind((arrays[0].shape[0], width), arrays[0].dtype) for width in widths],
        scratch_shapes=[pltpu.SemaphoreType.DMA((len(plan),))],
        compiler_params=params(),
        cost_estimate=LIGHT,
        name="columns",
    )(*arrays)


def load_kernel(step, a_ref, b_ref, a_out, b_out, gram_ref, sums, sem):
    columns = a_ref.shape[1]
    row = lax.broadcasted_iota(jnp.int32, (WIDE, WIDE), 0) // RANK
    col = lax.broadcasted_iota(jnp.int32, (WIDE, WIDE), 1) // RANK
    counts = [a_ref.shape[0] // step, b_ref.shape[0] // step]
    pairs = ((a_ref, a_out), (b_ref, b_out))

    def chunk(index, i):
        source, target = pairs[index]
        at = pl.ds(pl.multiple_of(i * step, step), step)
        return pltpu.make_async_copy(source.at[at], target.at[at], sem.at[index * counts[0] + i])

    for index in range(2):
        for i in range(counts[index]):
            chunk(index, i).start()
    for index in range(2):
        held = pairs[index][1]
        sums[...] = jnp.zeros_like(sums)

        @pl.loop(0, counts[index])
        def _(i, index=index, held=held):
            chunk(index, i).wait()
            for start in range(0, columns, WIDE):
                block = held[pl.ds(pl.multiple_of(i * step, step), step), start : start + WIDE]
                sums[:, start : start + WIDE] += lax.dot_general(
                    block, block, (((0,), (0,)), ((), ())), preferred_element_type=jnp.float32)

        for start in range(0, columns, WIDE):
            kept = jnp.where(row == col, sums[:, start : start + WIDE], 0.0)
            gram_ref[index, :, start : start + WIDE] = kept.reshape(WIDE // RANK, RANK, WIDE).sum(axis=0)


def load(a, b):
    columns = a.shape[1]
    step = chunk_of(math.gcd(a.shape[0], b.shape[0]))
    return pl.pallas_call(
        functools.partial(load_kernel, step),
        in_specs=[pl.BlockSpec(memory_space=pl.ANY)] * 2,
        out_specs=[pl.BlockSpec(memory_space=pltpu.VMEM)] * 3,
        out_shape=[
            pltpu.VMEM(a.shape, a.dtype), pltpu.VMEM(b.shape, b.dtype),
            jax.ShapeDtypeStruct((2, RANK, columns), jnp.float32)],
        scratch_shapes=[
            pltpu.VMEM((WIDE, columns), jnp.float32),
            pltpu.SemaphoreType.DMA(((a.shape[0] + b.shape[0]) // step,))],
        compiler_params=params(),
        cost_estimate=LIGHT,
        name="load_factors",
    )(in_hbm(a), in_hbm(b))


def pack_kernel(count, *refs):
    arrays, out_ref = refs[:count], refs[count]
    packed = jnp.concatenate([x[...] for x in arrays], axis=0)
    for copy in range(2):
        out_ref[copy] = packed


def twice(arrays):
    rows, width = sum(a.shape[0] for a in arrays), arrays[0].shape[1]
    step = chunk_of(width)
    return pl.pallas_call(
        functools.partial(pack_kernel, len(arrays)),
        grid=(width // step,),
        in_specs=[pl.BlockSpec((a.shape[0], step), lambda i: (0, i)) for a in arrays],
        out_specs=pl.BlockSpec((2, rows, step), lambda i: (0, 0, i)),
        out_shape=jax.ShapeDtypeStruct((2, rows, width), arrays[0].dtype),
        compiler_params=params(),
        cost_estimate=LIGHT,
        name="pack",
    )(*arrays)


def beside_kernel(*refs):
    arrays, out_ref, sem = refs[:-2], refs[-2], refs[-1]
    copies, put = [], 0
    for array in arrays:
        for copy in range(2):
            copies.append(pltpu.make_async_copy(
                array, out_ref.at[copy, :, pl.ds(put, array.shape[1])], sem.at[len(copies)]))
        put += array.shape[1]
    for copy in copies:
        copy.start()
    for copy in copies:
        copy.wait()


def beside_twice(arrays):
    shape = (2, arrays[0].shape[0], sum(a.shape[1] for a in arrays))
    return pl.pallas_call(
        beside_kernel,
        in_specs=[pl.BlockSpec(memory_space=pl.ANY)] * len(arrays),
        out_specs=pl.BlockSpec(memory_space=pl.ANY),
        out_shape=jax.ShapeDtypeStruct(shape, arrays[0].dtype),
        scratch_shapes=[pltpu.SemaphoreType.DMA((2 * len(arrays),))],
        compiler_params=params(),
        cost_estimate=LIGHT,
        name="pack",
    )(*arrays)


def project_kernel(step, spans, count, outs, more, *refs):
    held, factors = refs[:count], refs[count : count + 2]
    given, sums = refs[count + 2 : count + 2 + more], refs[-outs:]
    i = pl.program_id(0)
    rows = sums[0].shape[0]

    @pl.when(i == 0)
    def _():
        for index, out in enumerate(sums):
            if outs == 1 and more:
                out[...] = given[0][...]
            else:
                out[:rows] = jnp.zeros((rows, out.shape[1]), out.dtype)
        if outs == 2 and more:
            for j in range(2):
                sums[1][rows + j * RANK : rows + (j + 1) * RANK] = given[0][j]

    for begin, width, which, offset in spans:
        first, steps = begin // step, width // step

        @pl.when((i >= first) & (i < first + steps))
        def _(which=which, offset=offset, first=first):
            x = jnp.concatenate(
                [x for h in held for x in ((h[0], h[1]) if len(h.shape) == 3 else (h[...],))], axis=0)
            at = pl.multiple_of((i - first) * step + offset, step)
            sums[which if outs == 2 else 0][:rows] += jnp.dot(
                x, factors[which][pl.ds(at, step), :], preferred_element_type=jnp.float32)


def project(arrays, span, factors, outs, start=None):
    width = sum(size for _, size, _, _ in span)
    step = chunk_of(*(size for _, size, _, _ in span), most=3072)
    shape = (sum(math.prod(a.shape[:-1]) for a in arrays), factors[0].shape[1])
    extra = [] if start is None else [start]
    shapes = [shape] * outs
    if outs == 2 and extra:
        shapes[1] = (shape[0] + 2 * RANK, shape[1])
    result = pl.pallas_call(
        functools.partial(project_kernel, step, tuple(span), len(arrays), outs, len(extra)),
        grid=(width // step,),
        in_specs=[
            pl.BlockSpec((*a.shape[:-1], step), lambda i, zeros=(0,) * (a.ndim - 1): (*zeros, i)) for a in arrays]
        + [pl.BlockSpec(memory_space=pltpu.VMEM)] * (2 + len(extra)),
        out_specs=[pl.BlockSpec(x, lambda i: (0, 0)) for x in shapes],
        out_shape=[jax.ShapeDtypeStruct(x, jnp.float32) for x in shapes],
        compiler_params=params(),
        cost_estimate=LIGHT,
        name="project",
    )(*arrays, *[in_vmem(f) for f in factors], *extra)
    return result if outs == 2 else result[0]


def by_query(x):
    columns = x.shape[1]
    queries = columns // RANK
    member = (lax.broadcasted_iota(jnp.int32, (columns, queries), 0) // RANK) == lax.broadcasted_iota(
        jnp.int32, (columns, queries), 1)
    return jnp.dot(
        x, member.astype(jnp.float32), precision=lax.Precision.HIGHEST, preferred_element_type=jnp.float32)


def total_of(refs, rows=None):
    return sum(ref[:rows] for ref in refs[1:]) + refs[0][:rows]


def project_last_kernel(plan, counts, *refs):
    arrays, factors = refs[: counts[0]], refs[counts[0] : counts[0] + 2]
    starts, out_ref = refs[counts[0] + 2 : -1], refs[-1]
    if counts[1]:
        first = 0
        for start in starts:
            out_ref[first : first + start.shape[0]] = start[...]
            first += start.shape[0]
    else:
        out_ref[...] = jnp.zeros_like(out_ref)
    for held, width, which, offset in plan:
        step = chunk_of(width, most=5120)

        @pl.loop(0, width // step)
        def _(i, held=held, which=which, offset=offset, step=step):
            x = []
            for index, begin in held:
                at = pl.ds(pl.multiple_of(i * step + begin, 128), step)
                ref = arrays[index]
                x += [ref[0, :, at], ref[1, :, at]] if len(ref.shape) == 3 else [ref[:, at]]
            w = factors[which][pl.ds(pl.multiple_of(i * step + offset, 128), step), :]
            out_ref[...] += jnp.dot(jnp.concatenate(x, axis=0), w, preferred_element_type=jnp.float32)


def project_last(arrays, plan, factors, starts=()):
    rows = sum(math.prod(arrays[index].shape[:-1]) for index, _ in plan[0][0])
    given = [in_vmem(x) for x in (*arrays, *factors)] + list(starts)
    return pl.pallas_call(
        functools.partial(project_last_kernel, tuple(plan), (len(arrays), len(starts))),
        in_specs=[pl.BlockSpec(memory_space=pltpu.VMEM)] * len(given),
        out_specs=pl.BlockSpec(memory_space=pltpu.VMEM),
        out_shape=jax.ShapeDtypeStruct((rows, factors[0].shape[1]), jnp.float32),
        compiler_params=params(),
        cost_estimate=LIGHT,
        name="project_last",
    )(*given)


def score_kernel(first, rows, count, earlier, *refs):
    one, parts, out_ref = refs[earlier], refs[earlier + 1 : earlier + 1 + count], refs[-1]
    found = by_query(one[first : first + rows] * total_of(parts, rows)).T
    out_ref[...] = jnp.concatenate([*[ref[...] for ref in refs[:earlier]], found], axis=1)


def score(one, parts, earlier=(), first=0, rows=None):
    rows = rows or one.shape[0]
    return pl.pallas_call(
        functools.partial(score_kernel, first, rows, len(parts), len(earlier)),
        out_shape=jax.ShapeDtypeStruct(
            (one.shape[1] // RANK, rows + sum(x.shape[1] for x in earlier)), jnp.float32),
        compiler_params=params(),
        cost_estimate=LIGHT,
        name="score",
    )(*earlier, one, *parts)


def inverse_kernel(*refs):
    out_ref = refs[-1]
    gram = total_of(refs[:-1])
    first, second = (gram[0], gram[1]) if gram.ndim == 3 else (gram[-2 * RANK : -RANK], gram[-RANK:])
    norms = jnp.broadcast_to((first * second).sum(axis=0, keepdims=True), (8, gram.shape[-1]))
    inverse = 1.0 / jnp.sqrt(by_query(norms) + 1e-06)
    out_ref[...] = jnp.broadcast_to(inverse.T[:, :1], out_ref.shape)


def inverse_norms(parts):
    return pl.pallas_call(
        inverse_kernel,
        out_shape=jax.ShapeDtypeStruct((parts[0].shape[-1] // RANK, 128), jnp.float32),
        compiler_params=params(),
        cost_estimate=LIGHT,
        name="inverse_norms",
    )(*parts)


def looked_up(table, index):
    return sum(jnp.where(index == i, value, 0) for i, value in enumerate(table))


def last_kernel(groups, place, tokens, inverse_ref, *refs):
    out_ref = refs[-1]
    chips = len(place)
    scores = total_of(refs[:-1])
    width = scores.shape[1]
    starts = [[0] * chips for _ in range(2)]
    first = 0
    for group in groups:
        for c in range(2):
            for distance in group:
                starts[c][distance % chips] = first
                first += tokens
    query_at, side = lax.axis_index("query"), lax.axis_index("rows")
    core = query_at % 2
    here = looked_up(place, query_at // 2)
    share = out_ref.shape[1] // (2 * tokens)
    lane = lax.broadcasted_iota(jnp.int32, scores.shape, 1) // tokens
    result = jnp.zeros_like(scores)
    for j in range(share):
        distance = looked_up(place, side * share + j) - here
        distance = jnp.where(distance < 0, distance + chips, distance)
        firsts = [looked_up(starts[c], distance) for c in range(2)]
        turned = (distance == chips // 2) & (core == 1)
        firsts = [jnp.where(turned, firsts[1 - c], firsts[c]) for c in range(2)]
        for c in range(2):
            shift = (2 * j + c) * tokens - firsts[c]
            shift = jnp.where(shift < 0, shift + width, shift)
            result = jnp.where(lane == 2 * j + c, pltpu.roll(scores, shift, 1), result)
    out_ref[...] = result[:, : out_ref.shape[1]] * inverse_ref[:, :1]


def last(parts, inverse, groups, place, tokens, share):
    return pl.pallas_call(
        functools.partial(last_kernel, groups, place, tokens),
        in_specs=[pl.BlockSpec(memory_space=pltpu.VMEM)] * (1 + len(parts)),
        out_specs=pl.BlockSpec(memory_space=pltpu.VMEM),
        out_shape=jax.ShapeDtypeStruct((inverse.shape[0], share), jnp.float32),
        compiler_params=params(),
        cost_estimate=LIGHT,
        name="last_scores",
    )(inverse, *parts)


def solution(mesh):
    rows = mesh.shape["rows"]
    query = mesh.shape["query"]
    ring = ring_of(mesh)
    chips = len(ring)
    assert chips % 2 == 0 and chips >= 4
    forward = [(a, b) for i in range(chips) for a, b in zip(ring[i], ring[(i + 1) % chips])]
    backward = [(b, a) for a, b in forward]
    mates = [(pair[i], pair[1 - i]) for pair in ring for i in range(2)]
    place = [0] * chips
    for i, pair in enumerate(ring):
        place[pair[0] // 2] = i
    place = tuple(place)

    def across(x):
        if rows == 2:
            return [x, lax.ppermute(x, "rows", [(0, 1), (1, 0)])]
        return [lax.psum(x, "rows")]

    def both_cores(x):
        return lax.all_to_all(x, "query", 0, 0, axis_index_groups=sorted(ring))

    def mate(xs):
        return [lax.ppermute(x, "query", mates) for x in xs]

    def round_ring(pair):
        return [lax.ppermute(pair[0], "query", forward), lax.ppermute(pair[1], "query", backward)]

    def tied(*trees):
        return lax.optimization_barrier(trees)

    def local(acts, grads, in_factors, out_factors):
        tokens, width = acts.shape
        depth = grads.shape[1]
        half = (width + depth) // 256 * 128
        cut = half - depth
        assert cut > 0
        spans = [[(0, depth, 1, 0), (depth, cut, 0, 0)], [(0, width - cut, 0, cut)]]
        last_hop = chips // 2

        (own0,) = columns_of([in_hbm(grads), in_hbm(acts)], [[(0, 0, depth), (1, 0, cut)]], True)
        fly0 = round_ring([own0, own0])
        (own1,) = columns_of([in_hbm(acts)], [[(0, cut, width)]], True)
        fly1 = round_ring([own1, own1])
        *factors, gram = load(in_factors, out_factors)
        fly0, own0, own1, gram = tied(fly0, own0, own1, gram)
        groups, pair, found, gram_parts = [], [], [], []
        for hop in range(1, last_hop):
            extra = hop == 1
            final = hop + 1 == last_hop
            groups.append((-hop, hop) + (0,) * extra)
            held0 = fly0
            if final:
                middle, low = depth // 256 * 128, cut // 256 * 128
                fly0 = columns_of(held0, [
                    [(0, 0, middle), (0, depth, depth + low)], [(1, middle, depth), (1, depth + low, half)]], True)
            fly0 = round_ring(fly0)
            other, part = project(
                [both_cores(twice(held0 + [own0] * extra))], spans[0], factors, 2,
                gram if hop == 2 and not final else None)[::-1]
            if pair:
                part, pair, gram_parts = tied(part, pair, gram_parts)
                found = [score(pair[0], pair[1], found)]
            if final:
                inverse = inverse_norms(gram_parts or across(gram))
                found.append(inverse)
            fly1, other, part, found = tied(fly1, other, part, found)
            held1 = fly1
            if final:
                high = (width - cut) // 256 * 128 + (width - cut) // 24 // 128 * 128
                fly1 = columns_of(held1, [[(0, 0, high)], [(1, high, width - cut)]], True)
            fly1 = round_ring(fly1)
            swapped = both_cores(twice(held1 + [own1] * extra))
            if final:
                other = across(other)
                fly0, swapped, other, part = tied(fly0, swapped, other, part)
            else:
                one = project([swapped], spans[1], factors, 1, part)
                other = across(other)
                fly0, one, other = tied(fly0, one, other)
                pair = (one, other)
            if hop == 2 and not final:
                gram_parts = other
        groups.append((last_hop,))
        arrays = [swapped]
        held = columns_of(fly0, [
            [(0, 0, middle), (1, 0, depth - middle)],
            [(0, middle, middle + low)], [(1, depth - middle, half - middle - low)]], True)
        swapped = mate(held)
        last_other = project_last([held[0], swapped[0]], [(((0, 0), (1, 0)), depth, 1, 0)], factors)
        *found, inverse = found
        fly1, arrays, part, held, swapped, last_other, inverse, found = tied(
            fly1, arrays, part, held, swapped, last_other, inverse, found)
        last_part = project_last([*held[1:], *swapped[1:]], [
            (((0, 0), (2, 0)), low, 0, 0), (((1, 0), (3, 0)), cut - low, 0, low)], factors)
        swapped = mate(fly1)
        last_other = across(last_other)
        fly1, swapped, last_part = tied(fly1, swapped, last_part)
        one = project_last([*arrays, *fly1, *swapped], [
            (((0, 0), (1, 0), (3, 0)), high, 0, cut),
            (((0, high), (2, 0), (4, 0)), width - cut - high, 0, cut + high)], factors, [part, last_part])
        found = [score(one, other, found, 0, part.shape[0])]
        results = across(score(one, last_other, found, part.shape[0], 2 * tokens))
        return last(results, inverse, tuple(groups), place, tokens, query * tokens // rows).T

    return jax.shard_map(
        local,
        mesh=mesh,
        in_specs=(P("query", "rows"), P("query", "rows"), P("rows", "query"), P("rows", "query")),
        out_specs=P("rows", "query"),
        check_vma=False,
    )
```

```python
import functools
import math

import jax
import jax.numpy as jnp
from jax import lax
from jax.experimental import pallas as pl
from jax.experimental.pallas import tpu as pltpu
from jax.sharding import PartitionSpec as P

RANK = 32
WIDE = 256
LIGHT = pl.CostEstimate(flops=1, bytes_accessed=1, transcendentals=0)
ROOM = 6 << 20


def params():
    return pltpu.CompilerParams(vmem_limit_bytes=ROOM)


def in_hbm(x):
    return pltpu.with_memory_space_constraint(x, pltpu.HBM)


def in_vmem(x):
    return pltpu.with_memory_space_constraint(x, pltpu.VMEM)


def cycle_of(first, second):
    if min(first, second) == 1:
        size = first * second
        order = list(range(0, size, 2)) + list(range(1, size, 2))[::-1]
        return [(i, 0) if second == 1 else (0, i) for i in order]
    if first % 2:
        return [(a, b) for b, a in cycle_of(second, first)] if second % 2 == 0 else [
            (a, b) for a in range(first) for b in range(second)]
    walk = []
    for a in range(first):
        inner = range(1, second)
        walk += [(a, b) for b in (inner if a % 2 == 0 else reversed(inner))]
    return walk + [(a, 0) for a in reversed(range(first))]


def ring_of(mesh):
    devices = list(mesh.devices[0])
    chips = {}
    for index, device in enumerate(devices):
        coords = getattr(device, "coords", None)
        key = tuple(coords) if coords is not None else (index // 2,)
        chips.setdefault(key, []).append(index)
    keys = list(chips)
    values = [sorted({k[i] for k in keys}) for i in range(len(keys[0]))]
    varying = [i for i in range(len(values)) if len(values[i]) > 1]
    if len(varying) == 2 and len(keys) == len(values[varying[0]]) * len(values[varying[1]]):
        one, two = sorted(varying, key=lambda i: -len(values[i]))
        at = {(values[one].index(k[one]), values[two].index(k[two])): k for k in keys}
        keys = [at[place] for place in cycle_of(len(values[one]), len(values[two]))]
    ring = [chips[k] for k in keys]
    assert all(pair[0] % 2 == 0 and pair[1] == pair[0] + 1 for pair in ring)
    return ring


def chunk_of(*sizes, most=2048):
    whole = functools.reduce(math.gcd, sizes)
    return next(step for step in range(most, 0, -128) if whole % step == 0)


def copy_kernel(plan, count, *refs):
    sem = refs[-1]
    copies = [
        pltpu.make_async_copy(
            refs[source].at[:, pl.ds(begin, width)], refs[count + target].at[:, pl.ds(put, width)], sem.at[index])
        for index, (source, begin, target, put, width) in enumerate(plan)]
    for copy in copies:
        copy.start()
    for copy in copies:
        copy.wait()


def columns_of(arrays, outputs, vmem=False):
    kind, space = (pltpu.VMEM, pltpu.VMEM) if vmem else (jax.ShapeDtypeStruct, pl.ANY)
    plan, widths = [], []
    for target, ranges in enumerate(outputs):
        put = 0
        for source, lo, hi in ranges:
            plan.append((source, lo, target, put, hi - lo))
            put += hi - lo
        widths.append(put)
    return pl.pallas_call(
        functools.partial(copy_kernel, tuple(plan), len(arrays)),
        in_specs=[pl.BlockSpec(memory_space=pl.ANY)] * len(arrays),
        out_specs=[pl.BlockSpec(memory_space=space)] * len(outputs),
        out_shape=[kind((arrays[0].shape[0], width), arrays[0].dtype) for width in widths],
        scratch_shapes=[pltpu.SemaphoreType.DMA((len(plan),))],
        compiler_params=params(),
        cost_estimate=LIGHT,
        name="columns",
    )(*arrays)


def load_kernel(step, a_ref, b_ref, a_out, b_out, gram_ref, sums, sem):
    columns = a_ref.shape[1]
    row = lax.broadcasted_iota(jnp.int32, (WIDE, WIDE), 0) // RANK
    col = lax.broadcasted_iota(jnp.int32, (WIDE, WIDE), 1) // RANK
    counts = [a_ref.shape[0] // step, b_ref.shape[0] // step]
    pairs = ((a_ref, a_out), (b_ref, b_out))

    def chunk(index, i):
        source, target = pairs[index]
        at = pl.ds(pl.multiple_of(i * step, step), step)
        return pltpu.make_async_copy(source.at[at], target.at[at], sem.at[index * counts[0] + i])

    for index in range(2):
        for i in range(counts[index]):
            chunk(index, i).start()
    for index in range(2):
        held = pairs[index][1]
        sums[...] = jnp.zeros_like(sums)

        @pl.loop(0, counts[index])
        def _(i, index=index, held=held):
            chunk(index, i).wait()
            for start in range(0, columns, WIDE):
                block = held[pl.ds(pl.multiple_of(i * step, step), step), start : start + WIDE]
                sums[:, start : start + WIDE] += lax.dot_general(
                    block, block, (((0,), (0,)), ((), ())), preferred_element_type=jnp.float32)

        for start in range(0, columns, WIDE):
            kept = jnp.where(row == col, sums[:, start : start + WIDE], 0.0)
            gram_ref[index, :, start : start + WIDE] = kept.reshape(WIDE // RANK, RANK, WIDE).sum(axis=0)


def load(a, b):
    columns = a.shape[1]
    step = chunk_of(math.gcd(a.shape[0], b.shape[0]))
    return pl.pallas_call(
        functools.partial(load_kernel, step),
        in_specs=[pl.BlockSpec(memory_space=pl.ANY)] * 2,
        out_specs=[pl.BlockSpec(memory_space=pltpu.VMEM)] * 3,
        out_shape=[
            pltpu.VMEM(a.shape, a.dtype), pltpu.VMEM(b.shape, b.dtype),
            jax.ShapeDtypeStruct((2, RANK, columns), jnp.float32)],
        scratch_shapes=[
            pltpu.VMEM((WIDE, columns), jnp.float32),
            pltpu.SemaphoreType.DMA(((a.shape[0] + b.shape[0]) // step,))],
        compiler_params=params(),
        cost_estimate=LIGHT,
        name="load_factors",
    )(in_hbm(a), in_hbm(b))


def pack_kernel(count, *refs):
    arrays, out_ref = refs[:count], refs[count]
    packed = jnp.concatenate([x[...] for x in arrays], axis=0)
    for copy in range(2):
        out_ref[copy] = packed


def twice(arrays):
    rows, width = sum(a.shape[0] for a in arrays), arrays[0].shape[1]
    step = chunk_of(width)
    return pl.pallas_call(
        functools.partial(pack_kernel, len(arrays)),
        grid=(width // step,),
        in_specs=[pl.BlockSpec((a.shape[0], step), lambda i: (0, i)) for a in arrays],
        out_specs=pl.BlockSpec((2, rows, step), lambda i: (0, 0, i)),
        out_shape=jax.ShapeDtypeStruct((2, rows, width), arrays[0].dtype),
        compiler_params=params(),
        cost_estimate=LIGHT,
        name="pack",
    )(*arrays)


def beside_kernel(*refs):
    arrays, out_ref, sem = refs[:-2], refs[-2], refs[-1]
    copies, put = [], 0
    for array in arrays:
        for copy in range(2):
            copies.append(pltpu.make_async_copy(
                array, out_ref.at[copy, :, pl.ds(put, array.shape[1])], sem.at[len(copies)]))
        put += array.shape[1]
    for copy in copies:
        copy.start()
    for copy in copies:
        copy.wait()


def beside_twice(arrays):
    shape = (2, arrays[0].shape[0], sum(a.shape[1] for a in arrays))
    return pl.pallas_call(
        beside_kernel,
        in_specs=[pl.BlockSpec(memory_space=pl.ANY)] * len(arrays),
        out_specs=pl.BlockSpec(memory_space=pl.ANY),
        out_shape=jax.ShapeDtypeStruct(shape, arrays[0].dtype),
        scratch_shapes=[pltpu.SemaphoreType.DMA((2 * len(arrays),))],
        compiler_params=params(),
        cost_estimate=LIGHT,
        name="pack",
    )(*arrays)


def project_kernel(step, spans, count, outs, more, *refs):
    held, factors = refs[:count], refs[count : count + 2]
    given, sums = refs[count + 2 : count + 2 + more], refs[-outs:]
    i = pl.program_id(0)
    rows = sums[0].shape[0]

    @pl.when(i == 0)
    def _():
        for index, out in enumerate(sums):
            if outs == 1 and more:
                out[...] = given[0][...]
            else:
                out[:rows] = jnp.zeros((rows, out.shape[1]), out.dtype)
        if outs == 2 and more:
            for j in range(2):
                sums[1][rows + j * RANK : rows + (j + 1) * RANK] = given[0][j]

    for begin, width, which, offset in spans:
        first, steps = begin // step, width // step

        @pl.when((i >= first) & (i < first + steps))
        def _(which=which, offset=offset, first=first):
            x = jnp.concatenate(
                [x for h in held for x in ((h[0], h[1]) if len(h.shape) == 3 else (h[...],))], axis=0)
            at = pl.multiple_of((i - first) * step + offset, step)
            sums[which if outs == 2 else 0][:rows] += jnp.dot(
                x, factors[which][pl.ds(at, step), :], preferred_element_type=jnp.float32)


def project(arrays, span, factors, outs, start=None):
    width = sum(size for _, size, _, _ in span)
    step = chunk_of(*(size for _, size, _, _ in span), most=3072)
    shape = (sum(math.prod(a.shape[:-1]) for a in arrays), factors[0].shape[1])
    extra = [] if start is None else [start]
    shapes = [shape] * outs
    if outs == 2 and extra:
        shapes[1] = (shape[0] + 2 * RANK, shape[1])
    result = pl.pallas_call(
        functools.partial(project_kernel, step, tuple(span), len(arrays), outs, len(extra)),
        grid=(width // step,),
        in_specs=[
            pl.BlockSpec((*a.shape[:-1], step), lambda i, zeros=(0,) * (a.ndim - 1): (*zeros, i)) for a in arrays]
        + [pl.BlockSpec(memory_space=pltpu.VMEM)] * (2 + len(extra)),
        out_specs=[pl.BlockSpec(x, lambda i: (0, 0)) for x in shapes],
        out_shape=[jax.ShapeDtypeStruct(x, jnp.float32) for x in shapes],
        compiler_params=params(),
        cost_estimate=LIGHT,
        name="project",
    )(*arrays, *[in_vmem(f) for f in factors], *extra)
    return result if outs == 2 else result[0]


def by_query(x):
    columns = x.shape[1]
    queries = columns // RANK
    member = (lax.broadcasted_iota(jnp.int32, (columns, queries), 0) // RANK) == lax.broadcasted_iota(
        jnp.int32, (columns, queries), 1)
    return jnp.dot(
        x, member.astype(jnp.float32), precision=lax.Precision.HIGHEST, preferred_element_type=jnp.float32)


def total_of(refs, rows=None):
    return sum(ref[:rows] for ref in refs[1:]) + refs[0][:rows]


def project_last_kernel(plan, counts, *refs):
    arrays, factors = refs[: counts[0]], refs[counts[0] : counts[0] + 2]
    starts, out_ref = refs[counts[0] + 2 : -1], refs[-1]
    if counts[1]:
        first = 0
        for start in starts:
            out_ref[first : first + start.shape[0]] = start[...]
            first += start.shape[0]
    else:
        out_ref[...] = jnp.zeros_like(out_ref)
    for held, width, which, offset in plan:
        step = chunk_of(width, most=5120)

        @pl.loop(0, width // step)
        def _(i, held=held, which=which, offset=offset, step=step):
            x = []
            for index, begin in held:
                at = pl.ds(pl.multiple_of(i * step + begin, 128), step)
                ref = arrays[index]
                x += [ref[0, :, at], ref[1, :, at]] if len(ref.shape) == 3 else [ref[:, at]]
            w = factors[which][pl.ds(pl.multiple_of(i * step + offset, 128), step), :]
            out_ref[...] += jnp.dot(jnp.concatenate(x, axis=0), w, preferred_element_type=jnp.float32)


def project_last(arrays, plan, factors, starts=()):
    rows = sum(math.prod(arrays[index].shape[:-1]) for index, _ in plan[0][0])
    given = [in_vmem(x) for x in (*arrays, *factors)] + list(starts)
    return pl.pallas_call(
        functools.partial(project_last_kernel, tuple(plan), (len(arrays), len(starts))),
        in_specs=[pl.BlockSpec(memory_space=pltpu.VMEM)] * len(given),
        out_specs=pl.BlockSpec(memory_space=pltpu.VMEM),
        out_shape=jax.ShapeDtypeStruct((rows, factors[0].shape[1]), jnp.float32),
        compiler_params=params(),
        cost_estimate=LIGHT,
        name="project_last",
    )(*given)


def score_kernel(first, rows, count, earlier, *refs):
    one, parts, out_ref = refs[earlier], refs[earlier + 1 : earlier + 1 + count], refs[-1]
    found = by_query(one[first : first + rows] * total_of(parts, rows)).T
    out_ref[...] = jnp.concatenate([*[ref[...] for ref in refs[:earlier]], found], axis=1)


def score(one, parts, earlier=(), first=0, rows=None):
    rows = rows or one.shape[0]
    return pl.pallas_call(
        functools.partial(score_kernel, first, rows, len(parts), len(earlier)),
        out_shape=jax.ShapeDtypeStruct(
            (one.shape[1] // RANK, rows + sum(x.shape[1] for x in earlier)), jnp.float32),
        compiler_params=params(),
        cost_estimate=LIGHT,
        name="score",
    )(*earlier, one, *parts)


def inverse_kernel(*refs):
    out_ref = refs[-1]
    gram = total_of(refs[:-1])
    first, second = (gram[0], gram[1]) if gram.ndim == 3 else (gram[-2 * RANK : -RANK], gram[-RANK:])
    norms = jnp.broadcast_to((first * second).sum(axis=0, keepdims=True), (8, gram.shape[-1]))
    inverse = 1.0 / jnp.sqrt(by_query(norms) + 1e-06)
    out_ref[...] = jnp.broadcast_to(inverse.T[:, :1], out_ref.shape)


def inverse_norms(parts):
    return pl.pallas_call(
        inverse_kernel,
        out_shape=jax.ShapeDtypeStruct((parts[0].shape[-1] // RANK, 128), jnp.float32),
        compiler_params=params(),
        cost_estimate=LIGHT,
        name="inverse_norms",
    )(*parts)


def looked_up(table, index):
    return sum(jnp.where(index == i, value, 0) for i, value in enumerate(table))


def last_kernel(groups, place, tokens, inverse_ref, *refs):
    out_ref = refs[-1]
    chips = len(place)
    scores = total_of(refs[:-1])
    width = scores.shape[1]
    starts = [[0] * chips for _ in range(2)]
    first = 0
    for group in groups:
        for c in range(2):
            for distance in group:
                starts[c][distance % chips] = first
                first += tokens
    query_at, side = lax.axis_index("query"), lax.axis_index("rows")
    core = query_at % 2
    here = looked_up(place, query_at // 2)
    share = out_ref.shape[1] // (2 * tokens)
    lane = lax.broadcasted_iota(jnp.int32, scores.shape, 1) // tokens
    result = jnp.zeros_like(scores)
    for j in range(share):
        distance = looked_up(place, side * share + j) - here
        distance = jnp.where(distance < 0, distance + chips, distance)
        firsts = [looked_up(starts[c], distance) for c in range(2)]
        turned = (distance == chips // 2) & (core == 1)
        firsts = [jnp.where(turned, firsts[1 - c], firsts[c]) for c in range(2)]
        for c in range(2):
            shift = (2 * j + c) * tokens - firsts[c]
            shift = jnp.where(shift < 0, shift + width, shift)
            result = jnp.where(lane == 2 * j + c, pltpu.roll(scores, shift, 1), result)
    out_ref[...] = result[:, : out_ref.shape[1]] * inverse_ref[:, :1]


def last(parts, inverse, groups, place, tokens, share):
    return pl.pallas_call(
        functools.partial(last_kernel, groups, place, tokens),
        in_specs=[pl.BlockSpec(memory_space=pltpu.VMEM)] * (1 + len(parts)),
        out_specs=pl.BlockSpec(memory_space=pltpu.VMEM),
        out_shape=jax.ShapeDtypeStruct((inverse.shape[0], share), jnp.float32),
        compiler_params=params(),
        cost_estimate=LIGHT,
        name="last_scores",
    )(inverse, *parts)


def solution(mesh):
    rows = mesh.shape["rows"]
    query = mesh.shape["query"]
    ring = ring_of(mesh)
    chips = len(ring)
    assert chips % 2 == 0 and chips >= 4
    forward = [(a, b) for i in range(chips) for a, b in zip(ring[i], ring[(i + 1) % chips])]
    backward = [(b, a) for a, b in forward]
    mates = [(pair[i], pair[1 - i]) for pair in ring for i in range(2)]
    place = [0] * chips
    for i, pair in enumerate(ring):
        place[pair[0] // 2] = i
    place = tuple(place)

    def across(x):
        if rows == 2:
            return [x, lax.ppermute(x, "rows", [(0, 1), (1, 0)])]
        return [lax.psum(x, "rows")]

    def both_cores(x):
        return lax.all_to_all(x, "query", 0, 0, axis_index_groups=sorted(ring))

    def mate(xs):
        return [lax.ppermute(x, "query", mates) for x in xs]

    def round_ring(pair):
        return [lax.ppermute(pair[0], "query", forward), lax.ppermute(pair[1], "query", backward)]

    def tied(*trees):
        return lax.optimization_barrier(trees)

    def local(acts, grads, in_factors, out_factors):
        tokens, width = acts.shape
        depth = grads.shape[1]
        half = (width + depth) // 256 * 128
        cut = half - depth
        assert cut > 0
        spans = [[(0, depth, 1, 0), (depth, cut, 0, 0)], [(0, width - cut, 0, cut)]]
        last_hop = chips // 2

        (own0,) = columns_of([in_hbm(grads), in_hbm(acts)], [[(0, 0, depth), (1, 0, cut)]], True)
        fly0 = round_ring([own0, own0])
        (own1,) = columns_of([in_hbm(acts)], [[(0, cut, width)]], True)
        fly1 = round_ring([own1, own1])
        *factors, gram = load(in_factors, out_factors)
        fly0, own0, own1, gram = tied(fly0, own0, own1, gram)
        groups, pair, found, gram_parts = [], [], [], []
        for hop in range(1, last_hop):
            extra = hop == 1
            final = hop + 1 == last_hop
            groups.append((-hop, hop) + (0,) * extra)
            held0 = fly0
            if final:
                middle, low = depth // 256 * 128, cut // 256 * 128
                fly0 = columns_of(held0, [
                    [(0, 0, middle), (0, depth, depth + low)], [(1, middle, depth), (1, depth + low, half)]], True)
            fly0 = round_ring(fly0)
            other, part = project(
                [both_cores(twice(held0 + [own0] * extra))], spans[0], factors, 2,
                gram if hop == 2 and not final else None)[::-1]
            if pair:
                part, pair, gram_parts = tied(part, pair, gram_parts)
                found = [score(pair[0], pair[1], found)]
            if final:
                inverse = inverse_norms(gram_parts or across(gram))
                found.append(inverse)
            fly1, other, part, found = tied(fly1, other, part, found)
            held1 = fly1
            if final:
                high = (width - cut) // 256 * 128 + (width - cut) // 24 // 128 * 128
                fly1 = columns_of(held1, [[(0, 0, high)], [(1, high, width - cut)]], True)
            fly1 = round_ring(fly1)
            swapped = both_cores(twice(held1 + [own1] * extra))
            if final:
                other = across(other)
                fly0, swapped, other, part = tied(fly0, swapped, other, part)
            else:
                one = project([swapped], spans[1], factors, 1, part)
                other = across(other)
                fly0, one, other = tied(fly0, one, other)
                pair = (one, other)
            if hop == 2 and not final:
                gram_parts = other
        groups.append((last_hop,))
        arrays = [swapped]
        held = columns_of(fly0, [
            [(0, 0, middle), (1, 0, depth - middle)],
            [(0, middle, middle + low)], [(1, depth - middle, half - middle - low)]], True)
        swapped = mate(held)
        last_other = project_last([held[0], swapped[0]], [(((0, 0), (1, 0)), depth, 1, 0)], factors)
        *found, inverse = found
        fly1, arrays, part, held, swapped, last_other, inverse, found = tied(
            fly1, arrays, part, held, swapped, last_other, inverse, found)
        last_part = project_last([*held[1:], *swapped[1:]], [
            (((0, 0), (2, 0)), low, 0, 0), (((1, 0), (3, 0)), cut - low, 0, low)], factors)
        joined = columns_of(fly1, [[(0, 0, high), (1, 0, width - cut - high)]], True)
        swapped = mate(joined)
        last_other = across(last_other)
        joined, swapped, last_part = tied(joined, swapped, last_part)
        one = project_last([*arrays, *joined, *swapped], [
            (((0, 0), (1, 0), (2, 0)), width - cut, 0, cut)], factors, [part, last_part])
        found = [score(one, other, found, 0, part.shape[0])]
        results = across(score(one, last_other, found, part.shape[0], 2 * tokens))
        return last(results, inverse, tuple(groups), place, tokens, query * tokens // rows).T

    return jax.shard_map(
        local,
        mesh=mesh,
        in_specs=(P("query", "rows"), P("query", "rows"), P("rows", "query"), P("rows", "query")),
        out_specs=P("rows", "query"),
        check_vma=False,
    )
```

```python
import functools
import math

import jax
import jax.numpy as jnp
from jax import lax
from jax.experimental import pallas as pl
from jax.experimental.pallas import tpu as pltpu
from jax.sharding import PartitionSpec as P

RANK = 32
WIDE = 256
LIGHT = pl.CostEstimate(flops=1, bytes_accessed=1, transcendentals=0)
ROOM = 10 << 20


def params():
    return pltpu.CompilerParams(vmem_limit_bytes=ROOM)


def in_hbm(x):
    return pltpu.with_memory_space_constraint(x, pltpu.HBM)


def in_vmem(x):
    return pltpu.with_memory_space_constraint(x, pltpu.VMEM)


def cycle_of(first, second):
    if min(first, second) == 1:
        size = first * second
        order = list(range(0, size, 2)) + list(range(1, size, 2))[::-1]
        return [(i, 0) if second == 1 else (0, i) for i in order]
    if first % 2:
        return [(a, b) for b, a in cycle_of(second, first)] if second % 2 == 0 else [
            (a, b) for a in range(first) for b in range(second)]
    walk = []
    for a in range(first):
        inner = range(1, second)
        walk += [(a, b) for b in (inner if a % 2 == 0 else reversed(inner))]
    return walk + [(a, 0) for a in reversed(range(first))]


def ring_of(mesh):
    devices = list(mesh.devices[0])
    chips = {}
    for index, device in enumerate(devices):
        coords = getattr(device, "coords", None)
        key = tuple(coords) if coords is not None else (index // 2,)
        chips.setdefault(key, []).append(index)
    keys = list(chips)
    values = [sorted({k[i] for k in keys}) for i in range(len(keys[0]))]
    varying = [i for i in range(len(values)) if len(values[i]) > 1]
    if len(varying) == 2 and len(keys) == len(values[varying[0]]) * len(values[varying[1]]):
        one, two = sorted(varying, key=lambda i: -len(values[i]))
        at = {(values[one].index(k[one]), values[two].index(k[two])): k for k in keys}
        keys = [at[place] for place in cycle_of(len(values[one]), len(values[two]))]
    ring = [chips[k] for k in keys]
    assert all(pair[0] % 2 == 0 and pair[1] == pair[0] + 1 for pair in ring)
    return ring


def chunk_of(*sizes, most=2048):
    whole = functools.reduce(math.gcd, sizes)
    return next(step for step in range(most, 0, -128) if whole % step == 0)


def copy_kernel(plan, count, *refs):
    sem = refs[-1]
    copies = [
        pltpu.make_async_copy(
            refs[source].at[:, pl.ds(begin, width)], refs[count + target].at[:, pl.ds(put, width)], sem.at[index])
        for index, (source, begin, target, put, width) in enumerate(plan)]
    for copy in copies:
        copy.start()
    for copy in copies:
        copy.wait()


def columns_of(arrays, outputs, vmem=False):
    kind, space = (pltpu.VMEM, pltpu.VMEM) if vmem else (jax.ShapeDtypeStruct, pl.ANY)
    plan, widths = [], []
    for target, ranges in enumerate(outputs):
        put = 0
        for source, lo, hi in ranges:
            plan.append((source, lo, target, put, hi - lo))
            put += hi - lo
        widths.append(put)
    return pl.pallas_call(
        functools.partial(copy_kernel, tuple(plan), len(arrays)),
        in_specs=[pl.BlockSpec(memory_space=pl.ANY)] * len(arrays),
        out_specs=[pl.BlockSpec(memory_space=space)] * len(outputs),
        out_shape=[kind((arrays[0].shape[0], width), arrays[0].dtype) for width in widths],
        scratch_shapes=[pltpu.SemaphoreType.DMA((len(plan),))],
        compiler_params=params(),
        cost_estimate=LIGHT,
        name="columns",
    )(*arrays)


def load_kernel(step, a_ref, b_ref, a_out, b_out, gram_ref, sums, sem):
    columns = a_ref.shape[1]
    row = lax.broadcasted_iota(jnp.int32, (WIDE, WIDE), 0) // RANK
    col = lax.broadcasted_iota(jnp.int32, (WIDE, WIDE), 1) // RANK
    counts = [a_ref.shape[0] // step, b_ref.shape[0] // step]
    pairs = ((a_ref, a_out), (b_ref, b_out))

    def chunk(index, i):
        source, target = pairs[index]
        at = pl.ds(pl.multiple_of(i * step, step), step)
        return pltpu.make_async_copy(source.at[at], target.at[at], sem.at[index * counts[0] + i])

    for index in range(2):
        for i in range(counts[index]):
            chunk(index, i).start()
    for index in range(2):
        held = pairs[index][1]
        sums[...] = jnp.zeros_like(sums)

        @pl.loop(0, counts[index])
        def _(i, index=index, held=held):
            chunk(index, i).wait()
            for start in range(0, columns, WIDE):
                block = held[pl.ds(pl.multiple_of(i * step, step), step), start : start + WIDE]
                sums[:, start : start + WIDE] += lax.dot_general(
                    block, block, (((0,), (0,)), ((), ())), preferred_element_type=jnp.float32)

        for start in range(0, columns, WIDE):
            kept = jnp.where(row == col, sums[:, start : start + WIDE], 0.0)
            gram_ref[index, :, start : start + WIDE] = kept.reshape(WIDE // RANK, RANK, WIDE).sum(axis=0)


def load(a, b):
    columns = a.shape[1]
    step = chunk_of(math.gcd(a.shape[0], b.shape[0]))
    return pl.pallas_call(
        functools.partial(load_kernel, step),
        in_specs=[pl.BlockSpec(memory_space=pl.ANY)] * 2,
        out_specs=[pl.BlockSpec(memory_space=pltpu.VMEM)] * 3,
        out_shape=[
            pltpu.VMEM(a.shape, a.dtype), pltpu.VMEM(b.shape, b.dtype),
            jax.ShapeDtypeStruct((2, RANK, columns), jnp.float32)],
        scratch_shapes=[
            pltpu.VMEM((WIDE, columns), jnp.float32),
            pltpu.SemaphoreType.DMA(((a.shape[0] + b.shape[0]) // step,))],
        compiler_params=params(),
        cost_estimate=LIGHT,
        name="load_factors",
    )(in_hbm(a), in_hbm(b))


def pack_kernel(count, *refs):
    arrays, out_ref = refs[:count], refs[count]
    packed = jnp.concatenate([x[...] for x in arrays], axis=0)
    for copy in range(2):
        out_ref[copy] = packed


def twice(arrays):
    rows, width = sum(a.shape[0] for a in arrays), arrays[0].shape[1]
    step = chunk_of(width)
    return pl.pallas_call(
        functools.partial(pack_kernel, len(arrays)),
        grid=(width // step,),
        in_specs=[pl.BlockSpec((a.shape[0], step), lambda i: (0, i)) for a in arrays],
        out_specs=pl.BlockSpec((2, rows, step), lambda i: (0, 0, i)),
        out_shape=jax.ShapeDtypeStruct((2, rows, width), arrays[0].dtype),
        compiler_params=params(),
        cost_estimate=LIGHT,
        name="pack",
    )(*arrays)


def beside_kernel(*refs):
    arrays, out_ref, sem = refs[:-2], refs[-2], refs[-1]
    copies, put = [], 0
    for array in arrays:
        for copy in range(2):
            copies.append(pltpu.make_async_copy(
                array, out_ref.at[copy, :, pl.ds(put, array.shape[1])], sem.at[len(copies)]))
        put += array.shape[1]
    for copy in copies:
        copy.start()
    for copy in copies:
        copy.wait()


def beside_twice(arrays):
    shape = (2, arrays[0].shape[0], sum(a.shape[1] for a in arrays))
    return pl.pallas_call(
        beside_kernel,
        in_specs=[pl.BlockSpec(memory_space=pl.ANY)] * len(arrays),
        out_specs=pl.BlockSpec(memory_space=pl.ANY),
        out_shape=jax.ShapeDtypeStruct(shape, arrays[0].dtype),
        scratch_shapes=[pltpu.SemaphoreType.DMA((2 * len(arrays),))],
        compiler_params=params(),
        cost_estimate=LIGHT,
        name="pack",
    )(*arrays)


def project_kernel(step, spans, count, outs, more, *refs):
    held, factors = refs[:count], refs[count : count + 2]
    given, sums = refs[count + 2 : count + 2 + more], refs[-outs:]
    i = pl.program_id(0)
    rows = sums[0].shape[0]

    @pl.when(i == 0)
    def _():
        for index, out in enumerate(sums):
            if outs == 1 and more:
                out[...] = given[0][...]
            else:
                out[:rows] = jnp.zeros((rows, out.shape[1]), out.dtype)
        if outs == 2 and more:
            for j in range(2):
                sums[1][rows + j * RANK : rows + (j + 1) * RANK] = given[0][j]

    for begin, width, which, offset in spans:
        first, steps = begin // step, width // step

        @pl.when((i >= first) & (i < first + steps))
        def _(which=which, offset=offset, first=first):
            x = jnp.concatenate(
                [x for h in held for x in ((h[0], h[1]) if len(h.shape) == 3 else (h[...],))], axis=0)
            at = pl.multiple_of((i - first) * step + offset, step)
            sums[which if outs == 2 else 0][:rows] += jnp.dot(
                x, factors[which][pl.ds(at, step), :], preferred_element_type=jnp.float32)


def project(arrays, span, factors, outs, start=None):
    width = sum(size for _, size, _, _ in span)
    step = chunk_of(*(size for _, size, _, _ in span), most=4608)
    shape = (sum(math.prod(a.shape[:-1]) for a in arrays), factors[0].shape[1])
    extra = [] if start is None else [start]
    shapes = [shape] * outs
    if outs == 2 and extra:
        shapes[1] = (shape[0] + 2 * RANK, shape[1])
    result = pl.pallas_call(
        functools.partial(project_kernel, step, tuple(span), len(arrays), outs, len(extra)),
        grid=(width // step,),
        in_specs=[
            pl.BlockSpec((*a.shape[:-1], step), lambda i, zeros=(0,) * (a.ndim - 1): (*zeros, i)) for a in arrays]
        + [pl.BlockSpec(memory_space=pltpu.VMEM)] * (2 + len(extra)),
        out_specs=[pl.BlockSpec(x, lambda i: (0, 0)) for x in shapes],
        out_shape=[jax.ShapeDtypeStruct(x, jnp.float32) for x in shapes],
        compiler_params=params(),
        cost_estimate=LIGHT,
        name="project",
    )(*arrays, *[in_vmem(f) for f in factors], *extra)
    return result if outs == 2 else result[0]


def by_query(x):
    columns = x.shape[1]
    queries = columns // RANK
    member = (lax.broadcasted_iota(jnp.int32, (columns, queries), 0) // RANK) == lax.broadcasted_iota(
        jnp.int32, (columns, queries), 1)
    return jnp.dot(
        x, member.astype(jnp.float32), precision=lax.Precision.HIGHEST, preferred_element_type=jnp.float32)


def total_of(refs, rows=None):
    return sum(ref[:rows] for ref in refs[1:]) + refs[0][:rows]


def project_last_kernel(plan, counts, *refs):
    arrays, factors = refs[: counts[0]], refs[counts[0] : counts[0] + 2]
    starts, out_ref = refs[counts[0] + 2 : -1], refs[-1]
    if counts[1]:
        first = 0
        for start in starts:
            out_ref[first : first + start.shape[0]] = start[...]
            first += start.shape[0]
    else:
        out_ref[...] = jnp.zeros_like(out_ref)
    for held, width, which, offset in plan:
        step = chunk_of(width, most=5120)

        @pl.loop(0, width // step)
        def _(i, held=held, which=which, offset=offset, step=step):
            x = []
            for index, begin in held:
                at = pl.ds(pl.multiple_of(i * step + begin, 128), step)
                ref = arrays[index]
                x += [ref[0, :, at], ref[1, :, at]] if len(ref.shape) == 3 else [ref[:, at]]
            w = factors[which][pl.ds(pl.multiple_of(i * step + offset, 128), step), :]
            out_ref[...] += jnp.dot(jnp.concatenate(x, axis=0), w, preferred_element_type=jnp.float32)


def project_last(arrays, plan, factors, starts=()):
    rows = sum(math.prod(arrays[index].shape[:-1]) for index, _ in plan[0][0])
    given = [in_vmem(x) for x in (*arrays, *factors)] + list(starts)
    return pl.pallas_call(
        functools.partial(project_last_kernel, tuple(plan), (len(arrays), len(starts))),
        in_specs=[pl.BlockSpec(memory_space=pltpu.VMEM)] * len(given),
        out_specs=pl.BlockSpec(memory_space=pltpu.VMEM),
        out_shape=jax.ShapeDtypeStruct((rows, factors[0].shape[1]), jnp.float32),
        compiler_params=params(),
        cost_estimate=LIGHT,
        name="project_last",
    )(*given)


def score_kernel(first, rows, count, earlier, *refs):
    one, parts, out_ref = refs[earlier], refs[earlier + 1 : earlier + 1 + count], refs[-1]
    found = by_query(one[first : first + rows] * total_of(parts, rows)).T
    out_ref[...] = jnp.concatenate([*[ref[...] for ref in refs[:earlier]], found], axis=1)


def score(one, parts, earlier=(), first=0, rows=None):
    rows = rows or one.shape[0]
    return pl.pallas_call(
        functools.partial(score_kernel, first, rows, len(parts), len(earlier)),
        out_shape=jax.ShapeDtypeStruct(
            (one.shape[1] // RANK, rows + sum(x.shape[1] for x in earlier)), jnp.float32),
        compiler_params=params(),
        cost_estimate=LIGHT,
        name="score",
    )(*earlier, one, *parts)


def inverse_kernel(*refs):
    out_ref = refs[-1]
    gram = total_of(refs[:-1])
    first, second = (gram[0], gram[1]) if gram.ndim == 3 else (gram[-2 * RANK : -RANK], gram[-RANK:])
    norms = jnp.broadcast_to((first * second).sum(axis=0, keepdims=True), (8, gram.shape[-1]))
    inverse = 1.0 / jnp.sqrt(by_query(norms) + 1e-06)
    out_ref[...] = jnp.broadcast_to(inverse.T[:, :1], out_ref.shape)


def inverse_norms(parts):
    return pl.pallas_call(
        inverse_kernel,
        out_shape=jax.ShapeDtypeStruct((parts[0].shape[-1] // RANK, 128), jnp.float32),
        compiler_params=params(),
        cost_estimate=LIGHT,
        name="inverse_norms",
    )(*parts)


def looked_up(table, index):
    return sum(jnp.where(index == i, value, 0) for i, value in enumerate(table))


def last_kernel(groups, place, tokens, inverse_ref, *refs):
    out_ref = refs[-1]
    chips = len(place)
    scores = total_of(refs[:-1])
    width = scores.shape[1]
    starts = [[0] * chips for _ in range(2)]
    first = 0
    for group in groups:
        for c in range(2):
            for distance in group:
                starts[c][distance % chips] = first
                first += tokens
    query_at, side = lax.axis_index("query"), lax.axis_index("rows")
    core = query_at % 2
    here = looked_up(place, query_at // 2)
    share = out_ref.shape[1] // (2 * tokens)
    lane = lax.broadcasted_iota(jnp.int32, scores.shape, 1) // tokens
    result = jnp.zeros_like(scores)
    for j in range(share):
        distance = looked_up(place, side * share + j) - here
        distance = jnp.where(distance < 0, distance + chips, distance)
        firsts = [looked_up(starts[c], distance) for c in range(2)]
        turned = (distance == chips // 2) & (core == 1)
        firsts = [jnp.where(turned, firsts[1 - c], firsts[c]) for c in range(2)]
        for c in range(2):
            shift = (2 * j + c) * tokens - firsts[c]
            shift = jnp.where(shift < 0, shift + width, shift)
            result = jnp.where(lane == 2 * j + c, pltpu.roll(scores, shift, 1), result)
    out_ref[...] = result[:, : out_ref.shape[1]] * inverse_ref[:, :1]


def last(parts, inverse, groups, place, tokens, share):
    return pl.pallas_call(
        functools.partial(last_kernel, groups, place, tokens),
        in_specs=[pl.BlockSpec(memory_space=pltpu.VMEM)] * (1 + len(parts)),
        out_specs=pl.BlockSpec(memory_space=pltpu.VMEM),
        out_shape=jax.ShapeDtypeStruct((inverse.shape[0], share), jnp.float32),
        compiler_params=params(),
        cost_estimate=LIGHT,
        name="last_scores",
    )(inverse, *parts)


def solution(mesh):
    rows = mesh.shape["rows"]
    query = mesh.shape["query"]
    ring = ring_of(mesh)
    chips = len(ring)
    assert chips % 2 == 0 and chips >= 4
    forward = [(a, b) for i in range(chips) for a, b in zip(ring[i], ring[(i + 1) % chips])]
    backward = [(b, a) for a, b in forward]
    mates = [(pair[i], pair[1 - i]) for pair in ring for i in range(2)]
    place = [0] * chips
    for i, pair in enumerate(ring):
        place[pair[0] // 2] = i
    place = tuple(place)

    def across(x):
        if rows == 2:
            return [x, lax.ppermute(x, "rows", [(0, 1), (1, 0)])]
        return [lax.psum(x, "rows")]

    def both_cores(x):
        return lax.all_to_all(x, "query", 0, 0, axis_index_groups=sorted(ring))

    def mate(xs):
        return [lax.ppermute(x, "query", mates) for x in xs]

    def round_ring(pair):
        return [lax.ppermute(pair[0], "query", forward), lax.ppermute(pair[1], "query", backward)]

    def tied(*trees):
        return lax.optimization_barrier(trees)

    def local(acts, grads, in_factors, out_factors):
        tokens, width = acts.shape
        depth = grads.shape[1]
        half = (width + depth) // 256 * 128
        cut = half - depth
        assert cut > 0
        spans = [[(0, depth, 1, 0), (depth, cut, 0, 0)], [(0, width - cut, 0, cut)]]
        last_hop = chips // 2

        (own0,) = columns_of([in_hbm(grads), in_hbm(acts)], [[(0, 0, depth), (1, 0, cut)]], True)
        fly0 = round_ring([own0, own0])
        (own1,) = columns_of([in_hbm(acts)], [[(0, cut, width)]], True)
        fly1 = round_ring([own1, own1])
        *factors, gram = load(in_factors, out_factors)
        fly0, own0, own1, gram = tied(fly0, own0, own1, gram)
        groups, pair, found, gram_parts = [], [], [], []
        for hop in range(1, last_hop):
            extra = hop == 1
            final = hop + 1 == last_hop
            groups.append((-hop, hop) + (0,) * extra)
            held0 = fly0
            if final:
                middle, low = depth // 256 * 128, cut // 256 * 128
                fly0 = columns_of(held0, [
                    [(0, 0, middle), (0, depth, depth + low)], [(1, middle, depth), (1, depth + low, half)]], True)
            fly0 = round_ring(fly0)
            other, part = project(
                [both_cores(twice(held0 + [own0] * extra))], spans[0], factors, 2,
                gram if hop == 2 and not final else None)[::-1]
            if pair:
                part, pair, gram_parts = tied(part, pair, gram_parts)
                found = [score(pair[0], pair[1], found)]
            if final:
                inverse = inverse_norms(gram_parts or across(gram))
                found.append(inverse)
            fly1, other, part, found = tied(fly1, other, part, found)
            held1 = fly1
            if final:
                high = (width - cut) // 256 * 128 + (width - cut) // 24 // 128 * 128
                fly1 = columns_of(held1, [[(0, 0, high)], [(1, high, width - cut)]], True)
            fly1 = round_ring(fly1)
            swapped = both_cores(twice(held1 + [own1] * extra))
            if final:
                other = across(other)
                fly0, swapped, other, part = tied(fly0, swapped, other, part)
            else:
                one = project([swapped], spans[1], factors, 1, part)
                other = across(other)
                fly0, one, other = tied(fly0, one, other)
                pair = (one, other)
            if hop == 2 and not final:
                gram_parts = other
        groups.append((last_hop,))
        arrays = [swapped]
        held = columns_of(fly0, [
            [(0, 0, middle), (1, 0, depth - middle)],
            [(0, middle, middle + low)], [(1, depth - middle, half - middle - low)]], True)
        swapped = mate(held)
        last_other = project_last([held[0], swapped[0]], [(((0, 0), (1, 0)), depth, 1, 0)], factors)
        *found, inverse = found
        fly1, arrays, part, held, swapped, last_other, inverse, found = tied(
            fly1, arrays, part, held, swapped, last_other, inverse, found)
        last_part = project_last([*held[1:], *swapped[1:]], [
            (((0, 0), (2, 0)), low, 0, 0), (((1, 0), (3, 0)), cut - low, 0, low)], factors)
        swapped = mate(fly1)
        last_other = across(last_other)
        fly1, swapped, last_part = tied(fly1, swapped, last_part)
        one = project_last([*arrays, *fly1, *swapped], [
            (((0, 0), (1, 0), (3, 0)), high, 0, cut),
            (((0, high), (2, 0), (4, 0)), width - cut - high, 0, cut + high)], factors, [part, last_part])
        found = [score(one, other, found, 0, part.shape[0])]
        results = across(score(one, last_other, found, part.shape[0], 2 * tokens))
        return last(results, inverse, tuple(groups), place, tokens, query * tokens // rows).T

    return jax.shard_map(
        local,
        mesh=mesh,
        in_specs=(P("query", "rows"), P("query", "rows"), P("rows", "query"), P("rows", "query")),
        out_specs=P("rows", "query"),
        check_vma=False,
    )
```
